256 devices in a mesh: section: 2 (over core), expert: 128 (over z, y, x).
Axes of the slice: x: 4, y: 4, z: 8, core: 2. Of those that a mesh axis runs over, the one named last changes fastest.
Arguments:
- tokens_in: bfloat16 [2, 8192, 3584], P(None, 'expert'), may hold values from -6 to 6
- route_ids: int32 [2, 2, 8192, 1], P('section', None, 'expert'), may hold values from 0 to 63; in each aligned block of 64 rows (0 to 63, 64 to 127, ..., all dimensions but the last counted through in order) at most 2 rows name the same one
- norm_gain: bfloat16 [2, 3584], P('section', 'expert'), may hold values from 0.099609375 to 1.8984375
- router: bfloat16 [2, 3584, 64], P('section', 'expert'), may hold values from -0.1875 to 0.1875
- gate_proj: bfloat16 [2, 3584, 65536], P('section', None, 'expert'), may hold values from -0.09375 to 0.09375
- up_proj: bfloat16 [2, 3584, 65536], P('section', None, 'expert'), may hold values from -0.09375 to 0.09375
- down_proj: bfloat16 [2, 65536, 3584], P('section', 'expert'), may hold values from -0.1875 to 0.1875
Outputs:
- layer_out: bfloat16 [2, 2, 8192, 3584], P('section', None, 'expert')
The draws below stay inside these ranges and needn't reach their ends.
Inputs may be any that keep to these rules, and one draw needn't show every extreme that they name: `route_ids`: in each layer and micro-batch, the 64 tokens of one device (aligned blocks of 64 rows) name no expert more than 2 times, and in some of these blocks one expert exactly 2 times; the 1 ids of a token differ.
All inputs are finite; a program needn't handle non-finite values.
Results may differ from the reference program's by a relative error of at most 0.006.
Values may be sent and summed in bfloat16 or wider, within the bound.
A program may use at most 128 MiB of HBM per device.

```python
import math
import jax
import jax.numpy as jnp
import numpy as np
from jax import lax

D = 3584
HE = 1024
SPLIT = 2
TOPK = 1
MB = 2
TOK_DEV = 64
EXPERTS = 64
CAP = 2
TOKENS = 8192
N_EXPERT = 128


def block_levels(rng, extent, shards, low, high):
    gain = 1.0
    for axis_at, parts in shards:
        draws = jax.random.uniform(jax.random.fold_in(jax.random.fold_in(rng, 6), axis_at), (parts,), jnp.float32, low / len(shards), high / len(shards))
        gain = gain * jnp.repeat(jnp.exp(draws), extent[axis_at] // parts).reshape((-1,) + (1,) * (len(extent) - 1 - axis_at))
    return gain


def deal_out(key, own, number, rows, amount, top, most, lean):
    sequence = jax.random.permutation(key, amount)
    packed, usual = load_shares(amount, rows * top, most, lean, True), load_shares(amount, rows * top, most, lean, False)
    places = jnp.arange(amount)

    def named(sizes, turn):
        used = int((sizes > 0).sum())
        fixed = max(1, used // 4)
        shifted = fixed + (places - fixed + turn * (used - fixed)) % max(1, amount - fixed)
        return jnp.zeros((amount,), jnp.int32).at[sequence[jnp.where(places < fixed, places, shifted)]].set(jnp.asarray(sizes, jnp.int32))

    sizes = jnp.where(number % 4 == 0, named(packed, number // 4), named(usual, number - number // 4 - 1))
    mixed = jax.random.permutation(jax.random.fold_in(own, 3), amount)
    source_of, sink = mixed[0:amount // 2 * 2:2], mixed[1:amount // 2 * 2:2]
    margin = jnp.minimum(sizes[source_of] - 1, most - sizes[sink]) // 2
    margin = jnp.where((source_of == sequence[0]) | (sink == sequence[0]) | (sizes[sink] == 0), 0, jnp.maximum(margin, 0))
    shifted = jax.random.randint(jax.random.fold_in(own, 4), (amount // 2,), 0, 1 << 20) % (margin + 1)
    sizes = sizes.at[source_of].add(-shifted).at[sink].add(shifted)
    labels = jnp.searchsorted(jnp.cumsum(sizes), jnp.arange(rows * top), side="right").astype(jnp.int32)
    listing = labels.reshape(top, rows).T
    listing = listing[jax.random.permutation(jax.random.fold_in(own, 1), rows)]
    turn = jax.random.randint(jax.random.fold_in(own, 2), (rows, 1), 0, top)
    return jnp.take_along_axis(listing, (jnp.arange(top)[None, :] + turn) % top, axis=1)


def load_shares(amount, total, reach, skew, full):
    loads = [(1 << 20) // math.isqrt(standing ** skew) + 1 for standing in range(1, amount + 1)]
    largest = reach if full else min(reach, max(-(-total // amount), total * loads[0] // sum(loads)))
    least = 1 if total - largest >= amount - 1 else 0
    given, surplus = [largest] + [least] * (amount - 1), total - largest - least * (amount - 1)
    while surplus > 0:
        movable = [i for i in range(1, amount) if given[i] < largest] or [i for i in range(1, amount) if given[i] < reach]
        mass, budget = sum([loads[i] for i in movable]), surplus
        for i in movable:
            addition = min(reach - given[i], max(1, budget * loads[i] // mass), surplus)
            given[i] = given[i] + addition
            surplus = surplus - addition
    return np.array(given)


def bell_draw(stream_key, extent, deviation, reach, cuts=(), held_as=jnp.bfloat16):
    values = deviation * jax.random.normal(stream_key, extent, jnp.float32)
    if cuts:
        values = values * block_levels(stream_key, extent, cuts, -0.22, 0.18)
    return jnp.clip(values, -reach, reach).astype(held_as)


def setup_inputs(seed: int = 0) -> dict:
    streams_of = jax.random.split(jax.random.key(seed), 8)
    tokens_in = bell_draw(streams_of[0], (MB, TOKENS, D), 1.0, 6.0, ((1, 128),))
    route_ids_keys = jax.random.split(jax.random.fold_in(streams_of[1], 1), 2 * MB * TOKENS // TOK_DEV)
    route_ids_turns = jax.random.permutation(jax.random.fold_in(streams_of[1], 3), 2 * MB * TOKENS // TOK_DEV)
    route_ids = jax.vmap(lambda own, number: deal_out(jax.random.fold_in(streams_of[1], 2), own, number, TOK_DEV, EXPERTS, TOPK, CAP, 2))(route_ids_keys, route_ids_turns).reshape((2, MB, TOKENS, TOPK))
    norm_gain = jnp.clip(1.0 + 0.18 * jax.random.normal(streams_of[2], (2, D), jnp.float32), 0.099609375, 1.8984375).astype(jnp.bfloat16)
    router = bell_draw(streams_of[3], (2, D, EXPERTS), (D // 4) ** -0.5, 0.1875, ((0, 2), (1, 128)))
    gate_proj = bell_draw(streams_of[4], (2, D, EXPERTS * HE), D ** -0.5, 0.09375, ((0, 2), (2, 128)))
    up_proj = bell_draw(streams_of[5], (2, D, EXPERTS * HE), D ** -0.5, 0.09375, ((0, 2), (2, 128)))
    down_proj = bell_draw(streams_of[6], (2, EXPERTS * HE, D), HE ** -0.5, 0.1875, ((0, 2), (1, 128)))
    return dict(tokens_in=tokens_in, route_ids=route_ids, norm_gain=norm_gain, router=router, gate_proj=gate_proj, up_proj=up_proj, down_proj=down_proj)


def layer_apply(hidden, ids_row, gain_row, router_w, gate_w, up_w, down_w):
    widened = hidden.astype(jnp.float32)
    inv_rms = lax.rsqrt(lax.optimization_barrier(jnp.mean(widened * widened, axis=-1, keepdims=True)) + 1e-06)
    normed = (widened * inv_rms * gain_row.astype(jnp.float32)).astype(jnp.bfloat16)
    logits = jnp.dot(normed, router_w, preferred_element_type=jnp.float32)
    weights = jax.nn.sigmoid(jnp.take_along_axis(logits, ids_row, axis=1))
    flat_ids = ids_row.reshape(-1).astype(jnp.int32)
    sorted_order = jnp.argsort(flat_ids, stable=True).astype(jnp.int32)
    counts = lax.optimization_barrier(jnp.sum((flat_ids[:, None] == jnp.arange(EXPERTS, dtype=jnp.int32)[None, :]).astype(jnp.int32), axis=0)).astype(jnp.int32)
    starts = (jnp.cumsum(counts) - counts).astype(jnp.int32)
    row_limit = N_EXPERT * CAP
    sorted_tok = (sorted_order // TOPK).astype(jnp.int32)
    padded_tok = jnp.concatenate([sorted_tok, jnp.zeros((row_limit,), jnp.int32)])
    share = HE // SPLIT

    def one_expert(expert_index):
        begin = starts[expert_index]
        rows_idx = lax.dynamic_slice(padded_tok, (begin,), (row_limit,))
        rows_in = normed[rows_idx]
        column = (expert_index * HE).astype(jnp.int32)
        pre_gate = jnp.dot(rows_in, lax.dynamic_slice_in_dim(gate_w, column, HE, 1), preferred_element_type=jnp.float32)
        pre_up = jnp.dot(rows_in, lax.dynamic_slice_in_dim(up_w, column, HE, 1), preferred_element_type=jnp.float32)
        activated = (jax.nn.silu(pre_gate) * pre_up).astype(jnp.bfloat16)
        down_rows = lax.dynamic_slice_in_dim(down_w, column, HE, 0)
        total = jnp.zeros((row_limit, D), jnp.float32)
        for part_index in range(SPLIT):
            piece = jnp.dot(activated[:, part_index * share:(part_index + 1) * share], down_rows[part_index * share:(part_index + 1) * share], preferred_element_type=jnp.float32).astype(jnp.bfloat16)
            total = total + lax.optimization_barrier(piece).astype(jnp.float32)
        return total.astype(jnp.bfloat16)
    expert_all = lax.map(one_expert, jnp.arange(EXPERTS, dtype=jnp.int32))
    position = jnp.argsort(sorted_order, stable=True).astype(jnp.int32)
    offset = (position - starts[flat_ids]).astype(jnp.int32)
    expert_out = expert_all[flat_ids, offset].astype(jnp.float32).reshape(hidden.shape[0], TOPK, D)
    mixed_rows = widened + lax.optimization_barrier(jnp.sum(weights[:, :, None] * expert_out, axis=1))
    return mixed_rows.astype(jnp.bfloat16)

def reference(tokens_in, route_ids, norm_gain, router, gate_proj, up_proj, down_proj):
    layers = []
    current = tokens_in
    for layer_index in range(2):
        produced = []
        for micro_index in range(MB):
            produced.append(layer_apply(current[micro_index], route_ids[layer_index, micro_index], norm_gain[layer_index], router[layer_index], gate_proj[layer_index], up_proj[layer_index], down_proj[layer_index]))
        current = jnp.stack(produced)
        layers.append(current)
    return jnp.stack(layers)
```

```python
import jax
import jax.numpy as jnp
from jax import lax
from jax.sharding import PartitionSpec as P

HE = 1024


def shifted(block, axis, distance):
    devices = range(lax.axis_size(axis))
    route = [(i - distance, i) for i in devices if i - distance in devices]
    return lax.ppermute(block, axis, route)


def expert_rows(rows_in, gate_part, up_part, down_part):
    pre_gate = jnp.dot(rows_in, gate_part, preferred_element_type=jnp.float32)
    pre_up = jnp.dot(rows_in, up_part, preferred_element_type=jnp.float32)
    activated = (jax.nn.silu(pre_gate) * pre_up).astype(jnp.bfloat16)
    return jnp.dot(activated, down_part, preferred_element_type=jnp.float32).astype(jnp.bfloat16)


def on_device(tokens_in, route_ids, norm_gain, router, gate_proj, up_proj, down_proj):
    devices = lax.axis_size("expert")
    micro_count = tokens_in.shape[0]
    tok_rows = tokens_in.shape[1]
    model_width = tokens_in.shape[2]
    slice_units = gate_proj.shape[2]
    split_count = HE // slice_units
    expert_count = devices // split_count
    top_slots = route_ids.shape[3]
    capacity = 2 * tok_rows * top_slots // expert_count
    pair_count = tok_rows * top_slots
    section_index = lax.axis_index("section")
    share = jnp.concatenate([router[0], norm_gain[0][:, None]], axis=1)
    spread = jnp.broadcast_to(share[None], (devices,) + share.shape)
    gathered = lax.all_to_all(spread, "expert", split_axis=0, concat_axis=0, tiled=True)
    gathered = gathered.reshape(model_width, share.shape[1])
    gain_full, router_full = gathered[:, -1], gathered[:, :-1]
    gain_wide = gain_full.astype(jnp.float32)
    gate_part = gate_proj[0]
    up_part = up_proj[0]
    down_part = down_proj[0]
    slot_ids = jnp.arange(expert_count * capacity, dtype=jnp.int32)
    expert_ids = jnp.arange(expert_count, dtype=jnp.int32)

    def moe_layer(hidden_in, ids_now):
        widened = hidden_in.astype(jnp.float32)
        inv_rms = lax.rsqrt(jnp.mean(widened * widened, axis=-1, keepdims=True) + 1e-06)
        normed = (widened * inv_rms * gain_wide).astype(jnp.bfloat16)
        logits = jnp.dot(normed, router_full, preferred_element_type=jnp.float32)
        chosen = ids_now[:, :, None] == expert_ids[None, None, :]
        weights = jax.nn.sigmoid(jnp.sum(jnp.where(chosen, logits[:, None, :], 0.0), axis=-1))
        flat_hit = chosen.reshape(pair_count, expert_count).astype(jnp.int32)
        before = jnp.cumsum(flat_hit, axis=0) - flat_hit
        rank_in = jnp.sum(before * flat_hit, axis=-1)
        target = ids_now.reshape(pair_count) * capacity + rank_in
        placed = (
            (slot_ids[:, None] == target[None, :])
            .astype(jnp.bfloat16)
            .reshape(expert_count, capacity, pair_count)
        )
        pair_rows = normed[:, None, :].reshape(pair_count, model_width)
        outgoing = jnp.einsum(
            "ecp,pd->ecd", placed, pair_rows, preferred_element_type=jnp.float32
        ).astype(jnp.bfloat16)
        copies = jnp.broadcast_to(
            outgoing[:, None], (expert_count, split_count, capacity, model_width)
        ).reshape(devices * capacity, model_width)
        arrived = lax.all_to_all(copies, "expert", split_axis=0, concat_axis=0, tiled=True)
        partial_value = expert_rows(arrived, gate_part, up_part, down_part)
        returned = lax.all_to_all(partial_value, "expert", split_axis=0, concat_axis=0, tiled=True)
        summed = jnp.sum(
            returned.reshape(expert_count, split_count, capacity, model_width).astype(jnp.float32),
            axis=1,
        ).astype(jnp.bfloat16)
        expert_out = jnp.einsum("ecp,ecd->pd", placed, summed, preferred_element_type=jnp.float32)
        spread_out = expert_out.reshape(tok_rows, top_slots, model_width)
        mixed_rows = widened + jnp.sum(weights[:, :, None] * spread_out, axis=1)
        return mixed_rows.astype(jnp.bfloat16)

    ids_all = route_ids[0]
    first_pass = jnp.stack(
        [
            moe_layer(tokens_in[micro_index], ids_all[micro_index])
            for micro_index in range(micro_count)
        ]
    )
    moved_batch = shifted(first_pass, "section", 1)
    second = jnp.stack(
        [
            moe_layer(moved_batch[micro_index], ids_all[micro_index])
            for micro_index in range(micro_count)
        ]
    )
    result = jnp.where(section_index == 0, first_pass, second)
    return result[None]


def solution(mesh):
    return jax.shard_map(
        on_device,
        mesh=mesh,
        in_specs=(
            P(None, "expert", None),
            P("section", None, "expert", None),
            P("section", "expert"),
            P("section", "expert", None),
            P("section", None, "expert"),
            P("section", None, "expert"),
            P("section", "expert", None),
        ),
        out_specs=P("section", None, "expert", None),
        check_vma=False,
    )
```

```python
import functools

import jax
import jax.numpy as jnp
from jax import lax
from jax.experimental import pallas as pl
from jax.experimental.pallas import tpu as pltpu
from jax.sharding import PartitionSpec as P

MESH = pl.DeviceIdType.MESH
HE = 1024
MB = 2
RING_X, RING_Y, RING_Z = 4, 4, 8
PLANE = RING_Y * RING_Z
CHUNKS = 4
BF16 = jnp.bfloat16
F32 = jnp.float32


def landed(ref, sem):
    pltpu.make_async_copy(ref, ref, sem).wait()


def kernel(
    ids_ref, shared_ref, tokens_ref, gate_hbm, up_hbm, down_hbm, out_hbm,
    hidden, result, gate, up, down, place, unplace,
    outgo, arrive, across, acc_gate, acc_up, acc_logit, partial, partner_part, adj_sum, back, home,
    weight_sem, hidden_sem, out_sem, pass_sem, own_sem,
    out_send, out_recv, x_send, partner_recv, adj_recv, fwd_recv,
    part_send, part_recv, sum_send, sum_recv, home_send, home_recv, home_own,
):
    section = lax.axis_index("section")
    me = lax.axis_index("expert")
    x = lax.rem(me, RING_X)
    zy = me // RING_X
    y = lax.rem(zy, RING_Y)
    z = zy // RING_Y
    partner = x + 1 - 2 * lax.rem(x, 2)
    adjacent = 3 - x
    pair = x // 2
    tok_rows, width = hidden.shape[1], hidden.shape[2]
    chunk = width // CHUNKS
    slots = 4 * PLANE
    partner_id = {"expert": zy * RING_X + partner}
    adjacent_id = {"expert": zy * RING_X + adjacent}

    def peer(i):
        j = i // RING_Y
        dz = jnp.where(lax.rem(j, 2) == 1, (j + 1) // 2, RING_Z - j // 2)
        pz = lax.rem(z + dz, RING_Z)
        py = lax.rem(y + lax.rem(i, RING_Y), RING_Y)
        return pz * RING_Y + py

    weight_copies = [
        pltpu.make_async_copy(gate_hbm.at[0], gate, weight_sem.at[0]),
        pltpu.make_async_copy(up_hbm.at[0], up, weight_sem.at[1]),
        pltpu.make_async_copy(down_hbm.at[0], down, weight_sem.at[2]),
    ]

    @pl.when(section == 0)
    def _():
        for m in range(MB):
            pltpu.make_async_copy(tokens_ref.at[m], hidden.at[m], hidden_sem.at[m]).start()

    for copy in weight_copies:
        copy.start()

    barrier = pltpu.get_barrier_semaphore()

    def greet(i, carry):
        pl.semaphore_signal(
            barrier, inc=1, device_id={"expert": peer(i) * RING_X + x}, device_id_type=MESH
        )
        return carry

    lax.fori_loop(1, PLANE, greet, 0)
    for who in (partner_id, adjacent_id, {"section": 1 - section}):
        pl.semaphore_signal(barrier, inc=1, device_id=who, device_id_type=MESH)

    row_at = lax.broadcasted_iota(jnp.int32, (tok_rows, tok_rows), 0)
    col_at = lax.broadcasted_iota(jnp.int32, (tok_rows, tok_rows), 1)
    for m in range(MB):
        ids_row = ids_ref[pl.ds(m, 1), :]
        ids_mat = jnp.broadcast_to(ids_row, (tok_rows, tok_rows))
        ids_col = jnp.sum(jnp.where(row_at == col_at, ids_mat, 0), axis=1, keepdims=True)
        same = ids_mat == ids_col
        rank_row = jnp.sum(jnp.where(same & (row_at < col_at), 1, 0), axis=0, keepdims=True)
        rank_col = jnp.sum(jnp.where(same & (col_at < row_at), 1, 0), axis=1, keepdims=True)
        target_row = 2 * ids_row + rank_row
        target_col = 2 * ids_col + rank_col
        slot_at = lax.broadcasted_iota(jnp.int32, (slots, tok_rows), 0)
        place[m] = jnp.where(slot_at == target_row, 1.0, 0.0).astype(BF16)
        slot_at = lax.broadcasted_iota(jnp.int32, (tok_rows, slots), 1)
        unplace[m] = jnp.where(slot_at == target_col, 1.0, 0.0).astype(BF16)

    pl.semaphore_wait(barrier, PLANE + 2)

    def dispatch(m):
        landed(hidden.at[m], hidden_sem.at[m])
        wide = hidden[m].astype(F32)
        inv_rms = lax.rsqrt(jnp.mean(wide * wide, axis=-1, keepdims=True) + 1e-06)
        for c in range(CHUNKS):
            span = pl.ds(c * chunk, chunk)
            gain = shared_ref[0:1, span].astype(F32)
            normed = (hidden[m, :, span].astype(F32) * inv_rms * gain).astype(BF16)
            rows = jnp.dot(place[m], normed, preferred_element_type=F32).astype(BF16)
            outgo[m, c] = rows.reshape(PLANE, 2, 2, chunk)
            pltpu.make_async_copy(outgo.at[m, c, zy], arrive.at[m, c, zy], own_sem.at[m, c]).start()

            def send(i, carry):
                to = peer(i)
                pltpu.make_async_remote_copy(
                    src_ref=outgo.at[m, c, to],
                    dst_ref=arrive.at[m, c, zy],
                    send_sem=out_send.at[m, c],
                    recv_sem=out_recv.at[m, c],
                    device_id={"expert": to * RING_X + x},
                    device_id_type=MESH,
                ).start()
                return carry

            lax.fori_loop(1, PLANE, send, 0)

    def x_copy(src, dst, send_sem, recv_sem, who):
        return pltpu.make_async_remote_copy(
            src_ref=src, dst_ref=dst, send_sem=send_sem, recv_sem=recv_sem,
            device_id=who, device_id_type=MESH,
        )

    def to_partner(m, c):
        return x_copy(arrive.at[m, c, :, pair], across.at[m, c, 1], x_send.at[m, c, 0], partner_recv.at[m, c], partner_id)

    def to_adjacent(m, c):
        return x_copy(arrive.at[m, c, :, 1 - pair], across.at[m, c, 0], x_send.at[m, c, 1], adj_recv.at[m, c], adjacent_id)

    def forward(m, c):
        return x_copy(across.at[m, c, 0], across.at[m, c, 2], x_send.at[m, c, 2], fwd_recv.at[m, c], partner_id)

    def part_copy(m, c):
        return x_copy(partial.at[m, c, pl.ds(2, 2)], partner_part.at[m, c], part_send.at[m, c], part_recv.at[m, c], partner_id)

    def sum_copy(m, c):
        return x_copy(adj_sum.at[m, c], back.at[m, c, :, pair], sum_send.at[m, c], sum_recv.at[m, c], adjacent_id)

    def cross(m):
        for c in range(CHUNKS):
            landed(arrive.at[m, c, pl.ds(0, PLANE - 1)], out_recv.at[m, c])
            landed(arrive.at[m, c, 0], own_sem.at[m, c])
            to_adjacent(m, c).start()
            to_partner(m, c).start()
            if c > 0:
                landed(across.at[m, c - 1, 0], adj_recv.at[m, c - 1])
                forward(m, c - 1).start()
        landed(across.at[m, CHUNKS - 1, 0], adj_recv.at[m, CHUNKS - 1])
        forward(m, CHUNKS - 1).start()

    def experts(m):
        if m == 0:
            for copy in weight_copies:
                copy.wait()
        for c in range(CHUNKS):
            landed(across.at[m, c, 1], partner_recv.at[m, c])
            landed(across.at[m, c, 2], fwd_recv.at[m, c])
            span = pl.ds(c * chunk, chunk)
            own = arrive[m, c, :, pl.ds(pair, 1)].reshape(2 * PLANE, chunk)
            rows = jnp.concatenate([own, across[m, c].reshape(6 * PLANE, chunk)], axis=0)
            pre_gate = jnp.dot(rows, gate[span, :], preferred_element_type=F32)
            pre_up = jnp.dot(rows, up[span, :], preferred_element_type=F32)
            column = jnp.broadcast_to(shared_ref[1:2, span], (128, chunk))
            logit = lax.dot_general(rows, column, (((1,), (1,)), ((), ())), preferred_element_type=F32)
            if c == 0:
                acc_gate[...], acc_up[...], acc_logit[...] = pre_gate, pre_up, logit
            else:
                acc_gate[...] += pre_gate
                acc_up[...] += pre_up
                acc_logit[...] += logit
        pre_gate = acc_gate[...]
        activated = (pre_gate / (1.0 + jnp.exp(-pre_gate)) * acc_up[...]).astype(BF16)
        weight = 1.0 / (1.0 + jnp.exp(-acc_logit[:, 0:1]))
        for c in range(CHUNKS):
            span = pl.ds(c * chunk, chunk)
            part = jnp.dot(activated, down[:, span], preferred_element_type=F32) * weight
            partial[m, c] = part.astype(BF16).reshape(4, PLANE, 2, chunk)
            part_copy(m, c).start()

    def reduce(m):
        for c in range(CHUNKS):
            landed(partner_part.at[m, c], part_recv.at[m, c])
            for b in (1, 0):
                mine = partial[m, c, b].reshape(2 * PLANE, chunk).astype(F32)
                other = partner_part[m, c, b].reshape(2 * PLANE, chunk).astype(F32)
                total = (mine + other).astype(BF16).reshape(PLANE, 2, chunk)
                if b == 1:
                    adj_sum[m, c] = total
                    sum_copy(m, c).start()
                else:
                    back[m, c, :, pl.ds(pair, 1)] = total[:, None]

    def give_back(m):
        for c in range(CHUNKS):
            landed(adj_sum.at[m, c], sum_recv.at[m, c])
            pltpu.make_async_copy(back.at[m, c, zy], home.at[m, c, zy], home_own.at[m, c]).start()

            def send(i, carry):
                to = peer(i)
                pltpu.make_async_remote_copy(
                    src_ref=back.at[m, c, to],
                    dst_ref=home.at[m, c, zy],
                    send_sem=home_send.at[m, c],
                    recv_sem=home_recv.at[m, c],
                    device_id={"expert": to * RING_X + x},
                    device_id_type=MESH,
                ).start()
                return carry

            lax.fori_loop(1, PLANE, send, 0)

    def pass_on(m):
        return pltpu.make_async_remote_copy(
            src_ref=result.at[m], dst_ref=hidden.at[m], send_sem=pass_sem.at[m], recv_sem=hidden_sem.at[m],
            device_id={"section": 1}, device_id_type=MESH,
        )

    def combine(m):
        for c in range(CHUNKS):
            landed(home.at[m, c, pl.ds(0, PLANE - 1)], home_recv.at[m, c])
            landed(home.at[m, c, 0], home_own.at[m, c])
            span = pl.ds(c * chunk, chunk)
            spread = jnp.dot(unplace[m], home[m, c].reshape(slots, chunk), preferred_element_type=F32)
            result[m, :, span] = (hidden[m, :, span].astype(F32) + spread).astype(BF16)

        @pl.when(section == 0)
        def _():
            pass_on(m).start()

        pltpu.make_async_copy(result.at[m], out_hbm.at[m], out_sem.at[m]).start()

    dispatch(0)
    dispatch(1)
    for m in range(MB):
        cross(m)
        experts(m)
        reduce(m)
        give_back(m)
    for m in range(MB):
        combine(m)

    for m in range(MB):
        pltpu.make_async_copy(result.at[m], out_hbm.at[m], out_sem.at[m]).wait()

        @pl.when(section == 0)
        def _():
            pass_on(m).wait_send()

        for c in range(CHUNKS):
            landed(outgo.at[m, c, pl.ds(0, PLANE - 1)], out_send.at[m, c])
            landed(back.at[m, c, pl.ds(0, PLANE - 1)], home_send.at[m, c])
            to_partner(m, c).wait_send()
            to_adjacent(m, c).wait_send()
            forward(m, c).wait_send()
            part_copy(m, c).wait_send()
            sum_copy(m, c).wait_send()


def on_device(tokens_in, route_ids, norm_gain, router, gate_proj, up_proj, down_proj):
    devices = lax.axis_size("expert")
    micro_count, tok_rows, width = tokens_in.shape
    units = gate_proj.shape[2]
    share_width = norm_gain.shape[1]
    chunk = width // CHUNKS
    columns = jnp.repeat(router[0].T, HE // units, axis=0)
    gains = jnp.broadcast_to(norm_gain, (devices, share_width))
    spread = jnp.stack([gains, columns], axis=1)
    shared = lax.all_to_all(spread, "expert", split_axis=0, concat_axis=0, tiled=True)
    shared = shared.transpose(1, 0, 2).reshape(2, width)
    ids = route_ids.reshape(micro_count, tok_rows)
    any_space = pl.BlockSpec(memory_space=pl.ANY)
    vmem_space = pl.BlockSpec(memory_space=pltpu.VMEM)
    dma = pltpu.SemaphoreType.DMA
    grid = (MB, CHUNKS)
    out = pl.pallas_call(
        kernel,
        name="routed_experts",
        out_shape=jax.ShapeDtypeStruct((micro_count, tok_rows, width), BF16),
        in_specs=[vmem_space, vmem_space] + [any_space] * 4,
        out_specs=any_space,
        scratch_shapes=[
            pltpu.VMEM((MB, tok_rows, width), BF16),
            pltpu.VMEM((MB, tok_rows, width), BF16),
            pltpu.VMEM((width, units), BF16),
            pltpu.VMEM((width, units), BF16),
            pltpu.VMEM((units, width), BF16),
            pltpu.VMEM((MB, 4 * PLANE, tok_rows), BF16),
            pltpu.VMEM((MB, tok_rows, 4 * PLANE), BF16),
            pltpu.VMEM(grid + (PLANE, 2, 2, chunk), BF16),
            pltpu.VMEM(grid + (PLANE, 2, 2, chunk), BF16),
            pltpu.VMEM(grid + (3, PLANE, 2, chunk), BF16),
            pltpu.VMEM((8 * PLANE, units), F32),
            pltpu.VMEM((8 * PLANE, units), F32),
            pltpu.VMEM((8 * PLANE, 128), F32),
            pltpu.VMEM(grid + (4, PLANE, 2, chunk), BF16),
            pltpu.VMEM(grid + (2, PLANE, 2, chunk), BF16),
            pltpu.VMEM(grid + (PLANE, 2, chunk), BF16),
            pltpu.VMEM(grid + (PLANE, 2, 2, chunk), BF16),
            pltpu.VMEM(grid + (PLANE, 2, 2, chunk), BF16),
            dma((3,)), dma((MB,)), dma((MB,)), dma((MB,)), dma(grid),
            dma(grid), dma(grid), dma(grid + (3,)), dma(grid), dma(grid), dma(grid),
            dma(grid), dma(grid), dma(grid), dma(grid), dma(grid), dma(grid), dma(grid),
        ],
        compiler_params=pltpu.CompilerParams(
            collective_id=0, has_side_effects=True, vmem_limit_bytes=52 * 1024 * 1024
        ),
    )(ids, shared, tokens_in, gate_proj, up_proj, down_proj)
    return out[None]


def solution(mesh):
    return jax.shard_map(
        on_device,
        mesh=mesh,
        in_specs=(
            P(None, "expert", None),
            P("section", None, "expert", None),
            P("section", "expert"),
            P("section", "expert", None),
            P("section", None, "expert"),
            P("section", None, "expert"),
            P("section", "expert", None),
        ),
        out_specs=P("section", None, "expert", None),
        check_vma=False,
    )
```

```python
import functools

import jax
import jax.numpy as jnp
from jax import lax
from jax.experimental import pallas as pl
from jax.experimental.pallas import tpu as pltpu
from jax.sharding import PartitionSpec as P

MESH = pl.DeviceIdType.MESH
HE = 1024
MB = 2
RING_X, RING_Y, RING_Z = 4, 4, 8
PLANE = RING_Y * RING_Z
CHUNKS = 4
BF16 = jnp.bfloat16
F32 = jnp.float32
LANES = 128

FIRST = "P0 N00 N01 N02 N03"
SECOND = "P1 N10 N11 N12 N13"
ORDER = (
    "P1a N10a X00 N11a X01 N12a X02 N13a X03 G00 G01 X10a G02 X11a G03 A0 D00 D01 D02 D03 P1b N10b N11b N12b N13b "
    "X10b X11b X12 X13 S00 S01 S02 S03 G10 C00 G11 C01 G12 C02 G13 C03 A1 D10 D11 D12 D13 S10 S11 S12 S13 C10 C11 C12 C13"
)
ALL = tuple(range(CHUNKS))


def parse(names):
    return [(name[0], [int(digit) for digit in name[1:] if digit.isdigit()], name[-1]) for name in names.split()]


def landed(ref, sem):
    pltpu.make_async_copy(ref, ref, sem).wait()


def kernel(
    ids_ref, spread_ref, tokens_ref, gate_hbm, up_hbm, down_hbm, out_hbm,
    hidden, result, scale, gate, up, down, place, unplace, shares, shares_all, shared, selector,
    outgo, arrive, across, acc_gate, acc_up, acc_logit, active, partial, partner_part, back, home,
    weight_sem, hidden_sem, out_sem, pass_sem, own_sem, home_own,
    out_send, out_recv, x_send, x_recv, part_send, part_recv, home_send, home_recv,
    share_send, share_recv, share_x_send, share_x_recv,
):
    section = lax.axis_index("section")
    me = lax.axis_index("expert")
    x = lax.rem(me, RING_X)
    zy = me // RING_X
    y = lax.rem(zy, RING_Y)
    z = zy // RING_Y
    pair = x // 2
    partner = x + 1 - 2 * lax.rem(x, 2)
    adjacent = 3 - x
    far = lax.rem(x + 2, RING_X)
    tok_rows, width = hidden.shape[1], hidden.shape[2]
    chunk = width // CHUNKS
    slots = 4 * PLANE
    across_x = [{"expert": zy * RING_X + q} for q in (adjacent, partner, far)]

    def each_peer(act):
        def plane(j, skip_first):
            dz = jnp.where(lax.rem(j, 2) == 1, (j + 1) // 2, RING_Z - j // 2)
            first = lax.rem(z + dz, RING_Z) * RING_Y
            for dy in range(1 if skip_first else 0, RING_Y):
                act(first + lax.rem(y + dy, RING_Y))

        def body(j, carry):
            plane(j, False)
            return carry

        plane(0, True)
        lax.fori_loop(1, RING_Z, body, 0)

    def remote(src, dst, send_sem, recv_sem, who):
        return pltpu.make_async_remote_copy(
            src_ref=src, dst_ref=dst, send_sem=send_sem, recv_sem=recv_sem,
            device_id=who, device_id_type=MESH,
        )

    def to_plane(src, dst, send_sem, recv_sem, local_sem):
        pltpu.make_async_copy(src.at[zy], dst.at[zy], local_sem).start()

        each_peer(
            lambda to: remote(src.at[to], dst.at[zy], send_sem, recv_sem, {"expert": to * RING_X + x}).start()
        )

    def from_plane(dst, recv_sem, local_sem):
        landed(dst.at[pl.ds(0, PLANE - 1)], recv_sem)
        landed(dst.at[0], local_sem)

    weight_copies = [
        pltpu.make_async_copy(gate_hbm.at[0], gate, weight_sem.at[0]),
        pltpu.make_async_copy(up_hbm.at[0], up, weight_sem.at[1]),
        pltpu.make_async_copy(down_hbm.at[0], down, weight_sem.at[2]),
    ]

    @pl.when(section == 0)
    def _():
        for m in range(MB):
            pltpu.make_async_copy(tokens_ref.at[m], hidden.at[m], hidden_sem.at[m]).start()

    for copy in weight_copies:
        copy.start()

    barrier = pltpu.get_barrier_semaphore()

    each_peer(
        lambda to: pl.semaphore_signal(
            barrier, inc=1, device_id={"expert": to * RING_X + x}, device_id_type=MESH
        )
    )
    for who in across_x + [{"section": 1 - section}]:
        pl.semaphore_signal(barrier, inc=1, device_id=who, device_id_type=MESH)

    row_at = lax.broadcasted_iota(jnp.int32, (tok_rows, tok_rows), 0)
    col_at = lax.broadcasted_iota(jnp.int32, (tok_rows, tok_rows), 1)
    for m in range(MB):
        ids_row = ids_ref[pl.ds(m, 1), :]
        ids_mat = jnp.broadcast_to(ids_row, (tok_rows, tok_rows))
        ids_col = jnp.sum(jnp.where(row_at == col_at, ids_mat, 0), axis=1, keepdims=True)
        same = ids_mat == ids_col
        rank_row = jnp.sum(jnp.where(same & (row_at < col_at), 1, 0), axis=0, keepdims=True)
        rank_col = jnp.sum(jnp.where(same & (col_at < row_at), 1, 0), axis=1, keepdims=True)
        target_row = 2 * ids_row + rank_row
        target_col = 2 * ids_col + rank_col
        slot_at = lax.broadcasted_iota(jnp.int32, (slots, tok_rows), 0)
        place[m] = jnp.where(slot_at == target_row, 1.0, 0.0).astype(BF16)
        slot_at = lax.broadcasted_iota(jnp.int32, (tok_rows, slots), 1)
        unplace[m] = jnp.where(slot_at == target_col, 1.0, 0.0).astype(BF16)

    share_width = width // (RING_X * PLANE)
    column_at = lax.broadcasted_iota(jnp.int32, (1, width), 1)
    column_device = (column_at * ((1 << 18) // share_width + 1)) >> 18
    column_entry = column_at - column_device * share_width
    entry_at = lax.broadcasted_iota(jnp.int32, (LANES, width), 0)
    selector[...] = jnp.where(entry_at == column_entry, 1.0, 0.0).astype(BF16)

    shared[...] = jnp.zeros_like(shared)
    pl.semaphore_wait(barrier, PLANE + 3)
    to_plane(spread_ref, shares, share_send.at[0], share_recv.at[0], share_recv.at[1])

    def x_copies(src_of, dst, send_sems, recv_sem):
        return [remote(src_of(k), dst.at[k], send_sems.at[k], recv_sem, across_x[k]) for k in range(3)]

    share_copies = x_copies(
        lambda k: shares.at[:, pair if k == 1 else 1 - pair], shares_all.at[pl.ds(1, 3)], share_x_send, share_x_recv.at[0]
    )

    def pass_shares():
        from_plane(shares, share_recv.at[0], share_recv.at[1])
        for copy in share_copies:
            copy.start()
        shares_all[0] = shares[:, pl.ds(pair, 1)].reshape(PLANE, 2, LANES)

    def collect_shares():
        landed(shares_all.at[pl.ds(1, 3)], share_x_recv.at[0])
        blocks = shares_all[...].reshape(8 * PLANE, LANES)
        row = lax.broadcasted_iota(jnp.int32, (8 * PLANE, 1), 0)
        block = row // (2 * PLANE)
        row_x = jnp.where(block == 0, x, jnp.where(block == 1, adjacent, jnp.where(block == 2, partner, far)))
        row_device = lax.rem(row // 2, PLANE) * RING_X + row_x
        kind = lax.rem(lax.broadcasted_iota(jnp.int32, (8, 8 * PLANE), 1), 2)
        kinds = jnp.where(kind == lax.broadcasted_iota(jnp.int32, (8, 8 * PLANE), 0), 1.0, 0.0).astype(BF16)
        for c in ALL:
            span = pl.ds(c * chunk, chunk)
            entries = jnp.dot(blocks, selector[:, span], preferred_element_type=F32)
            device_of = (
                (lax.broadcasted_iota(jnp.int32, (1, chunk), 1) + c * chunk) * ((1 << 18) // share_width + 1)
            ) >> 18
            picked = jnp.where(row_device == device_of, entries, 0.0).astype(BF16)
            shared[:, span] = jnp.dot(kinds, picked, preferred_element_type=F32)

    def expert_gain(span):
        return jnp.where(section == 0, shared[0:1, span], 1.0).astype(BF16)

    def step_p(m):
        landed(hidden.at[m], hidden_sem.at[m])
        wide = hidden[m].astype(F32)
        inv_rms = lax.rsqrt(jnp.mean(wide * wide, axis=-1, keepdims=True) + 1e-06)
        scale[m] = jnp.broadcast_to(inv_rms, (tok_rows, LANES))

    def step_n(m, c, gained=True):
        span = pl.ds(c * chunk, chunk)
        normed = hidden[m, :, span].astype(F32) * scale[m, :, 0:1]
        if gained:
            normed = normed * shared[0:1, span]
        rows = jnp.dot(place[m], normed.astype(BF16), preferred_element_type=F32).astype(BF16)
        outgo[m, c] = rows.reshape(PLANE, 2, 2, chunk)
        to_plane(outgo.at[m, c], arrive.at[m, c], out_send.at[m, c], out_recv.at[m, c], own_sem.at[m, c])

    def share_rows(m, c):
        return x_copies(
            lambda k: arrive.at[m, c, :, pair if k == 1 else 1 - pair], across.at[m, c], x_send.at[m, c], x_recv.at[m, c]
        )

    def step_x(m, c):
        from_plane(arrive.at[m, c], out_recv.at[m, c], own_sem.at[m, c])
        for copy in share_rows(m, c):
            copy.start()

    def step_g(m, c):
        if m == 0 and c == 0:
            weight_copies[0].wait()
            weight_copies[1].wait()
        landed(across.at[m, c], x_recv.at[m, c])
        span = pl.ds(c * chunk, chunk)
        own = arrive[m, c, :, pl.ds(pair, 1)].reshape(2 * PLANE, chunk)
        rows = jnp.concatenate([own, across[m, c].reshape(6 * PLANE, chunk)], axis=0)
        rows = rows * expert_gain(span)
        pre_gate = jnp.dot(rows, gate[span, :], preferred_element_type=F32)
        pre_up = jnp.dot(rows, up[span, :], preferred_element_type=F32)
        column = jnp.broadcast_to(shared[1:2, span], (LANES, chunk)).astype(BF16)
        logit = lax.dot_general(rows, column, (((1,), (1,)), ((), ())), preferred_element_type=F32)
        if c == 0:
            acc_gate[...], acc_up[...], acc_logit[...] = pre_gate, pre_up, logit
        else:
            acc_gate[...] += pre_gate
            acc_up[...] += pre_up
            acc_logit[...] += logit

    def step_a(m):
        pre_gate = acc_gate[...]
        active[...] = (pre_gate / (1.0 + jnp.exp(-pre_gate)) * acc_up[...]).astype(BF16)
        if m == 0:
            weight_copies[2].wait()

    def part_copies(m, c):
        return [
            remote(partial.at[m, c, k + 1], partner_part.at[m, c, k], part_send.at[m, c, k], part_recv.at[m, c], across_x[k])
            for k in range(3)
        ]

    def step_d(m, c):
        weight = 1.0 / (1.0 + jnp.exp(-acc_logit[:, 0:1]))
        part = jnp.dot(active[...], down[:, pl.ds(c * chunk, chunk)], preferred_element_type=F32) * weight
        partial[m, c] = part.astype(BF16).reshape(4, PLANE, 2, chunk)
        for copy in part_copies(m, c):
            copy.start()

    def step_s(m, c):
        landed(partner_part.at[m, c], part_recv.at[m, c])

        def rows_of(ref):
            return ref[...].reshape(2 * PLANE, chunk).astype(F32)

        own = rows_of(partial.at[m, c, 0]) + rows_of(partner_part.at[m, c, 1])
        other = rows_of(partner_part.at[m, c, 0]) + rows_of(partner_part.at[m, c, 2])
        back[m, c, :, pl.ds(pair, 1)] = own.astype(BF16).reshape(PLANE, 1, 2, chunk)
        back[m, c, :, pl.ds(1 - pair, 1)] = other.astype(BF16).reshape(PLANE, 1, 2, chunk)
        to_plane(back.at[m, c], home.at[m, c], home_send.at[m, c], home_recv.at[m, c], home_own.at[m, c])

    def pass_on(m, c):
        piece = (m, slice(None), pl.ds(c * chunk, chunk))
        return remote(result.at[piece], hidden.at[piece], pass_sem.at[m], hidden_sem.at[m], {"section": 1})

    def out_copy(m, c):
        piece = (m, slice(None), pl.ds(c * chunk, chunk))
        return pltpu.make_async_copy(result.at[piece], out_hbm.at[piece], out_sem.at[m, c])

    def step_c(m, c):
        from_plane(home.at[m, c], home_recv.at[m, c], home_own.at[m, c])
        span = pl.ds(c * chunk, chunk)
        spread = jnp.dot(unplace[m], home[m, c].reshape(slots, chunk), preferred_element_type=F32)
        result[m, :, span] = (hidden[m, :, span].astype(F32) + spread).astype(BF16)
        pl.when(section == 0)(lambda: pass_on(m, c).start())
        out_copy(m, c).start()

    steps = dict(P=step_p, N=step_n, X=step_x, G=step_g, A=step_a, D=step_d, S=step_s, C=step_c)

    def run(names, **kind):
        for letter, numbers, only in parse(names):
            extra = {}
            if letter == "N":
                extra = dict(gained=False) if only == "a" else kind
            step = functools.partial(steps[letter], *numbers, **extra)
            if only in "ab":
                pl.when(section == "ab".index(only))(step)
            else:
                step()

    pl.when(section == 0)(lambda: run(FIRST, gained=False))
    pass_shares()

    @pl.when(section == 1)
    def _():
        collect_shares()
        run(FIRST)

    before, after = ORDER.split(" G00 ")
    run(before)
    pl.when(section == 0)(collect_shares)
    run("G00 " + after)

    landed(shares.at[pl.ds(0, PLANE - 1)], share_send.at[0])
    for copy in share_copies:
        copy.wait_send()
    for m in range(MB):
        pl.when(section == 0)(functools.partial(landed, result.at[m], pass_sem.at[m]))
        for c in ALL:
            landed(outgo.at[m, c, pl.ds(0, PLANE - 1)], out_send.at[m, c])
            for copy in share_rows(m, c) + part_copies(m, c):
                copy.wait_send()
            landed(back.at[m, c, pl.ds(0, PLANE - 1)], home_send.at[m, c])
            out_copy(m, c).wait()


def on_device(tokens_in, route_ids, norm_gain, router, gate_proj, up_proj, down_proj):
    micro_count, tok_rows, width = tokens_in.shape
    units = gate_proj.shape[2]
    share_width = norm_gain.shape[1]
    chunk = width // CHUNKS
    columns = router[0].T.reshape(PLANE, 2, 1, share_width)
    gains = jnp.broadcast_to(norm_gain, columns.shape)
    spread = jnp.pad(jnp.concatenate([gains, columns], axis=2), ((0, 0), (0, 0), (0, 0), (0, LANES - share_width)))
    ids = route_ids.reshape(micro_count, tok_rows)
    any_space = pl.BlockSpec(memory_space=pl.ANY)
    vmem_space = pl.BlockSpec(memory_space=pltpu.VMEM)
    dma = pltpu.SemaphoreType.DMA
    grid = (MB, CHUNKS)
    out = pl.pallas_call(
        kernel,
        name="routed_experts",
        out_shape=jax.ShapeDtypeStruct((micro_count, tok_rows, width), BF16),
        in_specs=[vmem_space, vmem_space] + [any_space] * 4,
        out_specs=any_space,
        scratch_shapes=[
            pltpu.VMEM((MB, tok_rows, width), BF16),
            pltpu.VMEM((MB, tok_rows, width), BF16),
            pltpu.VMEM((MB, tok_rows, LANES), F32),
            pltpu.VMEM((width, units), BF16),
            pltpu.VMEM((width, units), BF16),
            pltpu.VMEM((units, width), BF16),
            pltpu.VMEM((MB, 4 * PLANE, tok_rows), BF16),
            pltpu.VMEM((MB, tok_rows, 4 * PLANE), BF16),
            pltpu.VMEM((PLANE, 2, 2, LANES), BF16),
            pltpu.VMEM((4, PLANE, 2, LANES), BF16),
            pltpu.VMEM((8, width), F32),
            pltpu.VMEM((LANES, width), BF16),
            pltpu.VMEM(grid + (PLANE, 2, 2, chunk), BF16),
            pltpu.VMEM(grid + (PLANE, 2, 2, chunk), BF16),
            pltpu.VMEM(grid + (3, PLANE, 2, chunk), BF16),
            pltpu.VMEM((8 * PLANE, units), F32),
            pltpu.VMEM((8 * PLANE, units), F32),
            pltpu.VMEM((8 * PLANE, LANES), F32),
            pltpu.VMEM((8 * PLANE, units), BF16),
            pltpu.VMEM(grid + (4, PLANE, 2, chunk), BF16),
            pltpu.VMEM(grid + (3, PLANE, 2, chunk), BF16),
            pltpu.VMEM(grid + (PLANE, 2, 2, chunk), BF16),
            pltpu.VMEM(grid + (PLANE, 2, 2, chunk), BF16),
            dma((3,)), dma((MB,)), dma(grid), dma((MB,)), dma(grid), dma(grid),
            dma(grid), dma(grid), dma(grid + (3,)), dma(grid), dma(grid + (3,)), dma(grid), dma(grid), dma(grid),
            dma((1,)), dma((2,)), dma((3,)), dma((1,)),
        ],
        compiler_params=pltpu.CompilerParams(
            collective_id=0, has_side_effects=True, vmem_limit_bytes=52 * 1024 * 1024
        ),
    )(ids, spread, tokens_in, gate_proj, up_proj, down_proj)
    return out[None]


def solution(mesh):
    return jax.shard_map(
        on_device,
        mesh=mesh,
        in_specs=(
            P(None, "expert", None),
            P("section", None, "expert", None),
            P("section", "expert"),
            P("section", "expert", None),
            P("section", None, "expert"),
            P("section", None, "expert"),
            P("section", "expert", None),
        ),
        out_specs=P("section", None, "expert", None),
        check_vma=False,
    )
```

```python
import functools

import jax
import jax.numpy as jnp
from jax import lax
from jax.experimental import pallas as pl
from jax.experimental.pallas import tpu as pltpu
from jax.sharding import PartitionSpec as P

MESH = pl.DeviceIdType.MESH
HE = 1024
MB = 2
RING_X, RING_Y, RING_Z = 4, 4, 8
PLANE = RING_Y * RING_Z
CHUNKS = 2
BF16 = jnp.bfloat16
F32 = jnp.float32
LANES = 128

ALL = tuple(range(CHUNKS))
HALVES = (0, 1)
HALF = PLANE // 2
OWN = HALF - RING_Y
FIRST = ("N00a", "N01a", "M00a", "M01a")
ORDER = (
    "N00b", "M00b", "N01b", "M01b", "N10a", "N11a", "X000", "M10a", "X001a", "M11a", "X010", "X001b",
    "G000", "G010b", "G001", "A00", "X011", "D000", "D001", "G010a", "G011", "A01", "D010", "D011",
    "N10b", "M10b", "N11b", "M11b", "X100", "X110b", "X101", "X110a", "X111", "S000", "S001", "S010", "S011",
    "G100", "G101", "A10", "D100", "D101", "C00", "C01", "G110", "G111", "A11", "D110", "D111",
    "S100", "S101", "S110", "S111", "C10", "C11",
)


def parse(names):
    return [(name[0], [int(digit) for digit in name[1:] if digit.isdigit()], name[-1]) for name in names]


def landed(ref, sem):
    pltpu.make_async_copy(ref, ref, sem).wait()


def kernel(
    ids_hbm, spread_hbm, tokens_ref, gate_hbm, up_hbm, down_hbm, out_hbm,
    ids_ref, spread_ref, hidden, result, gate, up, down, place, unplace, shares, shares_all, shared, selector,
    outgo, arrive, across, acc_gate, acc_up, acc_logit, acc_square, weight, active, partial, partner_part, back, home,
    small_sem, weight_sem, hidden_sem, out_sem, pass_sem, own_sem, home_own,
    out_send, out_recv, x_send, x_recv, part_send, part_recv, home_send, home_recv,
    share_send, share_recv, share_x_send, share_x_recv,
):
    section = lax.axis_index("section")
    me = lax.axis_index("expert")
    x = lax.rem(me, RING_X)
    zy = me // RING_X
    y = lax.rem(zy, RING_Y)
    z = zy // RING_Y
    pair = x // 2
    partner = x + 1 - 2 * lax.rem(x, 2)
    adjacent = 3 - x
    far = lax.rem(x + 2, RING_X)
    tok_rows, width = hidden.shape[1], hidden.shape[2]
    chunk = width // CHUNKS
    slots = 4 * PLANE
    across_x = [{"expert": zy * RING_X + q} for q in (adjacent, partner, far)]

    def each_peer(half, act):
        def plane(k, dz, first):
            for dy in range(first, RING_Y):
                there = lax.rem(z + dz, RING_Z) * RING_Y + lax.rem(y + dy, RING_Y)
                thence = lax.rem(z + RING_Z - dz, RING_Z) * RING_Y + lax.rem(y + RING_Y - dy, RING_Y)
                act(k * RING_Y + dy, there, thence)

        def body(k, carry):
            plane(k, 2 * k + 2 - half, 0)
            return carry

        lax.fori_loop(0, RING_Z // 2 - 1 + half, body, 0)
        if half == 0:
            plane(RING_Z // 2 - 1, 0, 1)

    def remote(src, dst, send_sem, recv_sem, who):
        return pltpu.make_async_remote_copy(
            src_ref=src, dst_ref=dst, send_sem=send_sem, recv_sem=recv_sem,
            device_id=who, device_id_type=MESH,
        )

    def at_x(there):
        return {"expert": there * RING_X + x}

    def half_landed(dst, half, recv_sem, local_sem):
        landed(dst.at[pl.ds(0, HALF - 1 + half)], recv_sem)
        if half == 0:
            landed(dst.at[0], local_sem)

    weight_copies = [
        pltpu.make_async_copy(gate_hbm.at[0], gate, weight_sem.at[0]),
        pltpu.make_async_copy(up_hbm.at[0], up, weight_sem.at[1]),
        pltpu.make_async_copy(down_hbm.at[0], down, weight_sem.at[2]),
    ]

    ids_copy = pltpu.make_async_copy(ids_hbm, ids_ref, small_sem.at[0])
    spread_copy = pltpu.make_async_copy(spread_hbm, spread_ref, small_sem.at[1])
    ids_copy.start()
    spread_copy.start()

    @pl.when(section == 0)
    def _():
        for m in range(MB):
            for c in ALL:
                piece = (m, slice(None), pl.ds(c * chunk, chunk))
                pltpu.make_async_copy(tokens_ref.at[piece], hidden.at[piece], hidden_sem.at[m, c]).start()

    for copy in weight_copies:
        copy.start()

    barrier = pltpu.get_barrier_semaphore()

    for half in HALVES:
        each_peer(
            half,
            lambda i, there, thence: pl.semaphore_signal(
                barrier, inc=1, device_id=at_x(there), device_id_type=MESH
            ),
        )
    for who in across_x + [{"section": 1 - section}]:
        pl.semaphore_signal(barrier, inc=1, device_id=who, device_id_type=MESH)

    ids_copy.wait()
    row_at = lax.broadcasted_iota(jnp.int32, (tok_rows, tok_rows), 0)
    col_at = lax.broadcasted_iota(jnp.int32, (tok_rows, tok_rows), 1)
    for m in range(MB):
        ids_row = ids_ref[pl.ds(m, 1), :]
        ids_mat = jnp.broadcast_to(ids_row, (tok_rows, tok_rows))
        ids_col = jnp.sum(jnp.where(row_at == col_at, ids_mat, 0), axis=1, keepdims=True)
        same = ids_mat == ids_col
        rank_row = jnp.sum(jnp.where(same & (row_at < col_at), 1, 0), axis=0, keepdims=True)
        rank_col = jnp.sum(jnp.where(same & (col_at < row_at), 1, 0), axis=1, keepdims=True)
        target_row = 2 * ids_row + rank_row
        target_col = 2 * ids_col + rank_col
        slot_at = lax.broadcasted_iota(jnp.int32, (slots, tok_rows), 0)
        place[m] = jnp.where(slot_at == target_row, 1.0, 0.0).astype(BF16)
        slot_at = lax.broadcasted_iota(jnp.int32, (tok_rows, slots), 1)
        unplace[m] = jnp.where(slot_at == target_col, 1.0, 0.0).astype(BF16)

    share_width = width // (RING_X * PLANE)
    column_at = lax.broadcasted_iota(jnp.int32, (1, width), 1)
    column_device = (column_at * ((1 << 18) // share_width + 1)) >> 18
    column_entry = column_at - column_device * share_width
    entry_at = lax.broadcasted_iota(jnp.int32, (LANES, width), 0)
    selector[...] = jnp.where(entry_at == column_entry, 1.0, 0.0).astype(BF16)

    shared[...] = jnp.zeros_like(shared)
    pl.semaphore_wait(barrier, PLANE + 3)
    spread_copy.wait()
    shares[pl.ds(zy, 1)] = spread_ref[pl.ds(zy, 1)]
    for half in HALVES:
        each_peer(
            half,
            lambda i, there, thence: remote(
                spread_ref.at[there], shares.at[zy], share_send.at[0], share_recv.at[0], at_x(there)
            ).start(),
        )

    def x_copies(src_of, dst, send_sems, recv_sem):
        return [remote(src_of(k), dst.at[k], send_sems.at[k], recv_sem, across_x[k]) for k in range(3)]

    share_copies = x_copies(
        lambda k: shares.at[:, pair if k == 1 else 1 - pair], shares_all.at[pl.ds(1, 3)], share_x_send, share_x_recv.at[0]
    )

    def pass_shares():
        landed(shares.at[pl.ds(0, PLANE - 1)], share_recv.at[0])
        for copy in share_copies:
            copy.start()
        shares_all[0] = shares[:, pl.ds(pair, 1)].reshape(PLANE, 2, LANES)

    def collect_shares():
        landed(shares_all.at[pl.ds(1, 3)], share_x_recv.at[0])
        blocks = shares_all[...].reshape(8 * PLANE, LANES)
        row = lax.broadcasted_iota(jnp.int32, (8 * PLANE, 1), 0)
        block = row // (2 * PLANE)
        row_x = jnp.where(block == 0, x, jnp.where(block == 1, adjacent, jnp.where(block == 2, partner, far)))
        row_device = lax.rem(row // 2, PLANE) * RING_X + row_x
        kind = lax.rem(lax.broadcasted_iota(jnp.int32, (8, 8 * PLANE), 1), 2)
        kinds = jnp.where(kind == lax.broadcasted_iota(jnp.int32, (8, 8 * PLANE), 0), 1.0, 0.0).astype(BF16)
        for c in ALL:
            span = pl.ds(c * chunk, chunk)
            entries = jnp.dot(blocks, selector[:, span], preferred_element_type=F32)
            device_of = (
                (lax.broadcasted_iota(jnp.int32, (1, chunk), 1) + c * chunk) * ((1 << 18) // share_width + 1)
            ) >> 18
            picked = jnp.where(row_device == device_of, entries, 0.0).astype(BF16)
            shared[:, span] = jnp.dot(kinds, picked, preferred_element_type=F32)

    def step_n(m, c):
        span = pl.ds(c * chunk, chunk)
        landed(hidden.at[m, :, span], hidden_sem.at[m, c])
        rows = jnp.dot(place[m], hidden[m, :, span], preferred_element_type=F32).astype(BF16)
        outgo[m, c] = rows.reshape(PLANE, 2, 2, chunk)
        pltpu.make_async_copy(outgo.at[m, c, zy], arrive.at[m, 0, c, OWN], own_sem.at[m, c]).start()
        send_half(m, 0, c)

    def send_half(m, half, c):
        each_peer(
            half,
            lambda i, there, thence: remote(
                outgo.at[m, c, there], arrive.at[m, half, c, i], out_send.at[m, c], out_recv.at[m, half, c], at_x(there)
            ).start(),
        )

    def step_m(m, c):
        send_half(m, 1, c)

    def share_rows(m, half, c):
        return x_copies(
            lambda k: arrive.at[m, half, c, :, pair if k == 1 else 1 - pair],
            across.at[m, half, c], x_send.at[m, half, c], x_recv.at[m, half, c],
        )

    def step_x(m, half, c):
        half_landed(arrive.at[m, half, c], half, out_recv.at[m, half, c], own_sem.at[m, c])
        for copy in share_rows(m, half, c):
            copy.start()

    def step_g(m, half, c):
        if (m, half, c) == (0, 0, 0):
            weight_copies[0].wait()
            weight_copies[1].wait()
        landed(across.at[m, half, c], x_recv.at[m, half, c])
        span = pl.ds(c * chunk, chunk)
        own = arrive[m, half, c, :, pl.ds(pair, 1)].reshape(2 * HALF, chunk)
        rows = jnp.concatenate([own, across[m, half, c].reshape(6 * HALF, chunk)], axis=0)
        square = jnp.zeros((8 * HALF, LANES), F32)
        for lane in range(0, chunk, LANES):
            piece = rows[:, lane:lane + LANES].astype(F32)
            square += piece * piece
        rows = rows * shared[0:1, span].astype(BF16)
        pre_gate = jnp.dot(rows, gate[span, :], preferred_element_type=F32)
        pre_up = jnp.dot(rows, up[span, :], preferred_element_type=F32)
        column = jnp.broadcast_to(shared[1:2, span], (LANES, chunk)).astype(BF16)
        logit = lax.dot_general(rows, column, (((1,), (1,)), ((), ())), preferred_element_type=F32)
        if c == 0:
            acc_gate[half], acc_up[half], acc_logit[half], acc_square[half] = pre_gate, pre_up, logit, square
        else:
            acc_gate[half] += pre_gate
            acc_up[half] += pre_up
            acc_logit[half] += logit
            acc_square[half] += square

    def step_a(m, half):
        inv_rms = lax.rsqrt(jnp.sum(acc_square[half], axis=1, keepdims=True) * (1.0 / width) + 1e-06)
        pre_gate = acc_gate[half] * inv_rms
        active[half] = (pre_gate / (1.0 + jnp.exp(-pre_gate)) * (acc_up[half] * inv_rms)).astype(BF16)
        weight[half] = 1.0 / (1.0 + jnp.exp(-acc_logit[half] * inv_rms))
        if (m, half) == (0, 0):
            weight_copies[2].wait()

    def part_copies(m, half, c):
        return [
            remote(
                partial.at[m, half, c, k + 1], partner_part.at[m, half, c, k],
                part_send.at[m, half, c, k], part_recv.at[m, half, c], across_x[k],
            )
            for k in range(3)
        ]

    def step_d(m, half, c):
        part = jnp.dot(active[half], down[:, pl.ds(c * chunk, chunk)], preferred_element_type=F32) * weight[half, :, 0:1]
        partial[m, half, c] = part.astype(BF16).reshape(4, HALF, 2, chunk)
        for copy in part_copies(m, half, c):
            copy.start()

    def step_s(m, half, c):
        landed(partner_part.at[m, half, c], part_recv.at[m, half, c])

        def rows_of(ref):
            return ref[...].reshape(2 * HALF, chunk).astype(F32)

        own = rows_of(partial.at[m, half, c, 0]) + rows_of(partner_part.at[m, half, c, 1])
        other = rows_of(partner_part.at[m, half, c, 0]) + rows_of(partner_part.at[m, half, c, 2])
        back[m, half, c, :, pl.ds(pair, 1)] = own.astype(BF16).reshape(HALF, 1, 2, chunk)
        back[m, half, c, :, pl.ds(1 - pair, 1)] = other.astype(BF16).reshape(HALF, 1, 2, chunk)
        if half == 0:
            pltpu.make_async_copy(back.at[m, 0, c, OWN], home.at[m, c, zy], home_own.at[m, c]).start()
        each_peer(
            half,
            lambda i, there, thence: remote(
                back.at[m, half, c, i], home.at[m, c, zy], home_send.at[m, half, c], home_recv.at[m, half, c], at_x(thence)
            ).start(),
        )

    def pass_on(m, c):
        piece = (m, slice(None), pl.ds(c * chunk, chunk))
        return remote(result.at[piece], hidden.at[piece], pass_sem.at[m], hidden_sem.at[m, c], {"section": 1})

    def out_copy(m, c):
        piece = (m, slice(None), pl.ds(c * chunk, chunk))
        return pltpu.make_async_copy(result.at[piece], out_hbm.at[piece], out_sem.at[m, c])

    def step_c(m, c):
        for half in HALVES:
            half_landed(home.at[m, c], half, home_recv.at[m, half, c], home_own.at[m, c])
        span = pl.ds(c * chunk, chunk)
        spread = jnp.dot(unplace[m], home[m, c].reshape(slots, chunk), preferred_element_type=F32)
        result[m, :, span] = (hidden[m, :, span].astype(F32) + spread).astype(BF16)
        pl.when(section == 0)(lambda: pass_on(m, c).start())
        out_copy(m, c).start()

    steps = dict(N=step_n, M=step_m, X=step_x, G=step_g, A=step_a, D=step_d, S=step_s, C=step_c)

    def run(names):
        for letter, numbers, only in parse(names):
            step = functools.partial(steps[letter], *numbers)
            if only in "ab":
                pl.when(section == "ab".index(only))(step)
            else:
                step()

    begin = ORDER.index("G000")
    run(FIRST)
    pass_shares()
    run(ORDER[:begin])
    collect_shares()
    run(ORDER[begin:])

    landed(shares.at[pl.ds(0, PLANE - 1)], share_send.at[0])
    for copy in share_copies:
        copy.wait_send()
    for m in range(MB):
        pl.when(section == 0)(functools.partial(landed, result.at[m], pass_sem.at[m]))
        for c in ALL:
            landed(outgo.at[m, c, pl.ds(0, PLANE - 1)], out_send.at[m, c])
            for half in HALVES:
                for copy in share_rows(m, half, c) + part_copies(m, half, c):
                    copy.wait_send()
                landed(back.at[m, half, c, pl.ds(0, HALF - 1 + half)], home_send.at[m, half, c])
            out_copy(m, c).wait()


def on_device(tokens_in, route_ids, norm_gain, router, gate_proj, up_proj, down_proj):
    micro_count, tok_rows, width = tokens_in.shape
    units = gate_proj.shape[2]
    share_width = norm_gain.shape[1]
    chunk = width // CHUNKS
    columns = router[0].T.reshape(PLANE, 2, 1, share_width)
    gains = jnp.broadcast_to(norm_gain, columns.shape)
    spread = jnp.pad(jnp.concatenate([gains, columns], axis=2), ((0, 0), (0, 0), (0, 0), (0, LANES - share_width)))
    ids = route_ids.reshape(micro_count, tok_rows)
    any_space = pl.BlockSpec(memory_space=pl.ANY)
    dma = pltpu.SemaphoreType.DMA
    grid = (MB, 2, CHUNKS)
    out = pl.pallas_call(
        kernel,
        name="routed_experts",
        out_shape=jax.ShapeDtypeStruct((micro_count, tok_rows, width), BF16),
        in_specs=[any_space] * 6,
        out_specs=any_space,
        scratch_shapes=[
            pltpu.VMEM((MB, tok_rows), jnp.int32),
            pltpu.VMEM((PLANE, 2, 2, LANES), BF16),
            pltpu.VMEM((MB, tok_rows, width), BF16),
            pltpu.VMEM((MB, tok_rows, width), BF16),
            pltpu.VMEM((width, units), BF16),
            pltpu.VMEM((width, units), BF16),
            pltpu.VMEM((units, width), BF16),
            pltpu.VMEM((MB, 4 * PLANE, tok_rows), BF16),
            pltpu.VMEM((MB, tok_rows, 4 * PLANE), BF16),
            pltpu.VMEM((PLANE, 2, 2, LANES), BF16),
            pltpu.VMEM((4, PLANE, 2, LANES), BF16),
            pltpu.VMEM((8, width), F32),
            pltpu.VMEM((LANES, width), BF16),
            pltpu.VMEM((MB, CHUNKS, PLANE, 2, 2, chunk), BF16),
            pltpu.VMEM(grid + (HALF, 2, 2, chunk), BF16),
            pltpu.VMEM(grid + (3, HALF, 2, chunk), BF16),
            pltpu.VMEM((2, 8 * HALF, units), F32),
            pltpu.VMEM((2, 8 * HALF, units), F32),
            pltpu.VMEM((2, 8 * HALF, LANES), F32),
            pltpu.VMEM((2, 8 * HALF, LANES), F32),
            pltpu.VMEM((2, 8 * HALF, LANES), F32),
            pltpu.VMEM((2, 8 * HALF, units), BF16),
            pltpu.VMEM(grid + (4, HALF, 2, chunk), BF16),
            pltpu.VMEM(grid + (3, HALF, 2, chunk), BF16),
            pltpu.VMEM(grid + (HALF, 2, 2, chunk), BF16),
            pltpu.VMEM((MB, CHUNKS, PLANE, 2, 2, chunk), BF16),
            dma((2,)), dma((3,)), dma((MB, CHUNKS)), dma((MB, CHUNKS)), dma((MB,)), dma((MB, CHUNKS)), dma((MB, CHUNKS)),
            dma((MB, CHUNKS)), dma(grid), dma(grid + (3,)), dma(grid), dma(grid + (3,)), dma(grid), dma(grid), dma(grid),
            dma((1,)), dma((1,)), dma((3,)), dma((1,)),
        ],
        compiler_params=pltpu.CompilerParams(
            collective_id=0, has_side_effects=True, vmem_limit_bytes=52 * 1024 * 1024
        ),
    )(ids, spread, tokens_in, gate_proj, up_proj, down_proj)
    return out[None]


def solution(mesh):
    return jax.shard_map(
        on_device,
        mesh=mesh,
        in_specs=(
            P(None, "expert", None),
            P("section", None, "expert", None),
            P("section", "expert"),
            P("section", "expert", None),
            P("section", None, "expert"),
            P("section", None, "expert"),
            P("section", "expert", None),
        ),
        out_specs=P("section", None, "expert", None),
        check_vma=False,
    )
```

```python
import functools

import jax
import jax.numpy as jnp
from jax import lax
from jax.experimental import pallas as pl
from jax.experimental.pallas import tpu as pltpu
from jax.sharding import PartitionSpec as P

MESH = pl.DeviceIdType.MESH
HE = 1024
MB = 2
RING_X, RING_Y, RING_Z = 4, 4, 8
PLANE = RING_Y * RING_Z
CHUNKS = 2
VMEM_BYTES = 64 * 1024 * 1024
BF16 = jnp.bfloat16
F32 = jnp.float32
LANES = 128

ALL = tuple(range(CHUNKS))
HALVES = (0, 1)
HALF = PLANE // 2
OWN = HALF - RING_Y
FIRST = ("N00a", "N01a", "M00a", "M01a")
ORDER = (
    "N00b", "M00b", "N01b", "M01b", "N10a", "N11a", "X000", "M10a", "X001a", "M11a", "X010", "X001b",
    "G000", "G010b", "G001", "A00", "X011", "D000", "D001", "G010a", "G011", "A01", "D010", "D011",
    "N10b", "M10b", "N11b", "M11b", "X100", "X110b", "X101", "X110a", "X111", "S000", "S001", "S010", "S011",
    "G100", "G101", "A10", "D100", "D101", "C00", "C01", "G110", "G111", "A11", "D110", "D111",
    "S100", "S101", "S110", "S111", "C10", "C11",
)


def parse(names):
    return [(name[0], [int(digit) for digit in name[1:] if digit.isdigit()], name[-1]) for name in names]


def landed(ref, sem):
    pltpu.make_async_copy(ref, ref, sem).wait()


def kernel(
    ids_hbm, gain_hbm, router_hbm, tokens_ref, gate_hbm, up_hbm, down_hbm, out_hbm,
    ids_ref, gain_ref, router_ref, spread_ref, hidden, result, gate, up, down, place, unplace, shares, shares_all, shared, selector,
    outgo, arrive, across, acc_gate, acc_up, acc_logit, acc_square, weight, active, partial, partner_part, back, home,
    small_sem, weight_sem, hidden_sem, out_sem, pass_sem, own_sem, home_own,
    out_send, out_recv, x_send, x_recv, part_send, part_recv, home_send, home_recv,
    share_send, share_recv, share_x_send, share_x_recv,
):
    section = lax.axis_index("section")
    me = lax.axis_index("expert")
    x = lax.rem(me, RING_X)
    zy = me // RING_X
    y = lax.rem(zy, RING_Y)
    z = zy // RING_Y
    pair = x // 2
    partner = x + 1 - 2 * lax.rem(x, 2)
    adjacent = 3 - x
    far = lax.rem(x + 2, RING_X)
    tok_rows, width = hidden.shape[1], hidden.shape[2]
    chunk = width // CHUNKS
    slots = 4 * PLANE
    across_x = [{"expert": zy * RING_X + q} for q in (adjacent, partner, far)]

    def each_peer(half, act):
        def plane(k, dz, first):
            for dy in range(first, RING_Y):
                there = lax.rem(z + dz, RING_Z) * RING_Y + lax.rem(y + dy, RING_Y)
                thence = lax.rem(z + RING_Z - dz, RING_Z) * RING_Y + lax.rem(y + RING_Y - dy, RING_Y)
                act(k * RING_Y + dy, there, thence)

        def body(k, carry):
            plane(k, 2 * k + 2 - half, 0)
            return carry

        lax.fori_loop(0, RING_Z // 2 - 1 + half, body, 0)
        if half == 0:
            plane(RING_Z // 2 - 1, 0, 1)

    def remote(src, dst, send_sem, recv_sem, who):
        return pltpu.make_async_remote_copy(
            src_ref=src, dst_ref=dst, send_sem=send_sem, recv_sem=recv_sem,
            device_id=who, device_id_type=MESH,
        )

    def at_x(there):
        return {"expert": there * RING_X + x}

    def half_landed(dst, half, recv_sem, local_sem):
        landed(dst.at[pl.ds(0, HALF - 1 + half)], recv_sem)
        if half == 0:
            landed(dst.at[0], local_sem)

    weight_copies = [
        pltpu.make_async_copy(gate_hbm.at[0], gate, weight_sem.at[0]),
        pltpu.make_async_copy(up_hbm.at[0], up, weight_sem.at[1]),
        pltpu.make_async_copy(down_hbm.at[0], down, weight_sem.at[2]),
    ]

    ids_copy = pltpu.make_async_copy(ids_hbm, ids_ref, small_sem.at[0])
    gain_copy = pltpu.make_async_copy(gain_hbm, gain_ref, small_sem.at[1])
    router_copy = pltpu.make_async_copy(router_hbm.at[0], router_ref, small_sem.at[2])
    for copy in (ids_copy, gain_copy, router_copy):
        copy.start()

    @pl.when(section == 0)
    def _():
        for m in range(MB):
            for c in ALL:
                piece = (m, slice(None), pl.ds(c * chunk, chunk))
                pltpu.make_async_copy(tokens_ref.at[piece], hidden.at[piece], hidden_sem.at[m, c]).start()

    for copy in weight_copies:
        copy.start()

    barrier = pltpu.get_barrier_semaphore()

    for half in HALVES:
        each_peer(
            half,
            lambda i, there, thence: pl.semaphore_signal(
                barrier, inc=1, device_id=at_x(there), device_id_type=MESH
            ),
        )
    for who in across_x + [{"section": 1 - section}]:
        pl.semaphore_signal(barrier, inc=1, device_id=who, device_id_type=MESH)

    ids_copy.wait()
    row_at = lax.broadcasted_iota(jnp.int32, (tok_rows, tok_rows), 0)
    col_at = lax.broadcasted_iota(jnp.int32, (tok_rows, tok_rows), 1)
    for m in range(MB):
        ids_row = ids_ref[pl.ds(m, 1), :]
        ids_mat = jnp.broadcast_to(ids_row, (tok_rows, tok_rows))
        ids_col = jnp.sum(jnp.where(row_at == col_at, ids_mat, 0), axis=1, keepdims=True)
        same = ids_mat == ids_col
        rank_row = jnp.sum(jnp.where(same & (row_at < col_at), 1, 0), axis=0, keepdims=True)
        rank_col = jnp.sum(jnp.where(same & (col_at < row_at), 1, 0), axis=1, keepdims=True)
        target_row = 2 * ids_row + rank_row
        target_col = 2 * ids_col + rank_col
        slot_at = lax.broadcasted_iota(jnp.int32, (slots, tok_rows), 0)
        place[m] = jnp.where(slot_at == target_row, 1.0, 0.0).astype(BF16)
        slot_at = lax.broadcasted_iota(jnp.int32, (tok_rows, slots), 1)
        unplace[m] = jnp.where(slot_at == target_col, 1.0, 0.0).astype(BF16)

    share_width = width // (RING_X * PLANE)
    column_at = lax.broadcasted_iota(jnp.int32, (1, width), 1)
    column_device = (column_at * ((1 << 18) // share_width + 1)) >> 18
    column_entry = column_at - column_device * share_width
    entry_at = lax.broadcasted_iota(jnp.int32, (LANES, width), 0)
    selector[...] = jnp.where(entry_at == column_entry, 1.0, 0.0).astype(BF16)

    gain_copy.wait()
    router_copy.wait()
    rows, columns = 4 * PLANE, LANES
    widen = jnp.where(
        lax.broadcasted_iota(jnp.int32, (columns, share_width), 0) == lax.broadcasted_iota(jnp.int32, (columns, share_width), 1),
        1.0, 0.0,
    ).astype(BF16)
    router_wide = jnp.dot(widen, router_ref[...], preferred_element_type=F32).astype(BF16)
    gain_rows = jnp.broadcast_to(gain_ref[...], (8, share_width))
    gain_wide = lax.dot_general(gain_rows, widen, (((1,), (1,)), ((), ())), preferred_element_type=F32)
    experts = router_ref.shape[1]
    row_at = lax.broadcasted_iota(jnp.int32, (rows, experts), 0)
    expert_at = lax.broadcasted_iota(jnp.int32, (rows, experts), 1)
    expert_rows = jnp.where(row_at == 2 * expert_at + 1, 1.0, 0.0).astype(BF16)
    router_rows = lax.dot_general(expert_rows, router_wide, (((1,), (1,)), ((), ())), preferred_element_type=F32)
    kind = lax.rem(lax.broadcasted_iota(jnp.int32, (rows, columns), 0), 2)
    spread = jnp.where(kind == 0, gain_wide[0:1, :], router_rows)
    spread_ref[...] = spread.astype(BF16).reshape(PLANE, 2, 2, LANES)
    pl.semaphore_wait(barrier, PLANE + 3)
    shares[pl.ds(zy, 1)] = spread_ref[pl.ds(zy, 1)]
    for half in HALVES:
        each_peer(
            half,
            lambda i, there, thence: remote(
                spread_ref.at[there], shares.at[zy], share_send.at[0], share_recv.at[0], at_x(there)
            ).start(),
        )

    def x_copies(src_of, dst, send_sems, recv_sem):
        return [remote(src_of(k), dst.at[k], send_sems.at[k], recv_sem, across_x[k]) for k in range(3)]

    share_copies = x_copies(
        lambda k: shares.at[:, pair if k == 1 else 1 - pair], shares_all.at[pl.ds(1, 3)], share_x_send, share_x_recv.at[0]
    )

    def pass_shares():
        landed(shares.at[pl.ds(0, PLANE - 1)], share_recv.at[0])
        for copy in share_copies:
            copy.start()
        shares_all[0] = shares[:, pl.ds(pair, 1)].reshape(PLANE, 2, LANES)

    def collect_shares():
        landed(shares_all.at[pl.ds(1, 3)], share_x_recv.at[0])
        blocks = shares_all[...].reshape(8 * PLANE, LANES)
        row = lax.broadcasted_iota(jnp.int32, (8 * PLANE, 1), 0)
        block = row // (2 * PLANE)
        row_x = jnp.where(block == 0, x, jnp.where(block == 1, adjacent, jnp.where(block == 2, partner, far)))
        row_device = lax.rem(row // 2, PLANE) * RING_X + row_x
        kind = lax.rem(lax.broadcasted_iota(jnp.int32, (8, 8 * PLANE), 1), 2)
        kinds = jnp.where(kind == lax.broadcasted_iota(jnp.int32, (8, 8 * PLANE), 0), 1.0, 0.0).astype(BF16)
        for c in ALL:
            span = pl.ds(c * chunk, chunk)
            entries = jnp.dot(blocks, selector[:, span], preferred_element_type=F32)
            device_of = (
                (lax.broadcasted_iota(jnp.int32, (1, chunk), 1) + c * chunk) * ((1 << 18) // share_width + 1)
            ) >> 18
            picked = jnp.where(row_device == device_of, entries, 0.0).astype(BF16)
            shared[:, span] = jnp.dot(kinds, picked, preferred_element_type=F32)

    def step_n(m, c):
        span = pl.ds(c * chunk, chunk)
        landed(hidden.at[m, :, span], hidden_sem.at[m, c])
        rows = jnp.dot(place[m], hidden[m, :, span], preferred_element_type=F32).astype(BF16)
        outgo[m, c] = rows.reshape(PLANE, 2, 2, chunk)
        pltpu.make_async_copy(outgo.at[m, c, zy], arrive.at[m, 0, c, OWN], own_sem.at[m, c]).start()
        send_half(m, 0, c)

    def send_half(m, half, c):
        each_peer(
            half,
            lambda i, there, thence: remote(
                outgo.at[m, c, there], arrive.at[m, half, c, i], out_send.at[m, c], out_recv.at[m, half, c], at_x(there)
            ).start(),
        )

    def step_m(m, c):
        send_half(m, 1, c)

    def share_rows(m, half, c):
        return x_copies(
            lambda k: arrive.at[m, half, c, :, pair if k == 1 else 1 - pair],
            across.at[m, half, c], x_send.at[m, half, c], x_recv.at[m, half, c],
        )

    def step_x(m, half, c):
        half_landed(arrive.at[m, half, c], half, out_recv.at[m, half, c], own_sem.at[m, c])
        for copy in share_rows(m, half, c):
            copy.start()

    def step_g(m, half, c):
        if (m, half, c) == (0, 0, 0):
            weight_copies[0].wait()
            weight_copies[1].wait()
        landed(across.at[m, half, c], x_recv.at[m, half, c])
        span = pl.ds(c * chunk, chunk)
        own = arrive[m, half, c, :, pl.ds(pair, 1)].reshape(2 * HALF, chunk)
        rows = jnp.concatenate([own, across[m, half, c].reshape(6 * HALF, chunk)], axis=0)
        square = jnp.zeros((8 * HALF, LANES), F32)
        for lane in range(0, chunk, LANES):
            piece = rows[:, lane:lane + LANES].astype(F32)
            square += piece * piece
        rows = rows * shared[0:1, span].astype(BF16)
        pre_gate = jnp.dot(rows, gate[span, :], preferred_element_type=F32)
        pre_up = jnp.dot(rows, up[span, :], preferred_element_type=F32)
        column = jnp.broadcast_to(shared[1:2, span], (LANES, chunk)).astype(BF16)
        logit = lax.dot_general(rows, column, (((1,), (1,)), ((), ())), preferred_element_type=F32)
        if c == 0:
            acc_gate[half], acc_up[half], acc_logit[half], acc_square[half] = pre_gate, pre_up, logit, square
        else:
            acc_gate[half] += pre_gate
            acc_up[half] += pre_up
            acc_logit[half] += logit
            acc_square[half] += square

    def step_a(m, half):
        inv_rms = lax.rsqrt(jnp.sum(acc_square[half], axis=1, keepdims=True) * (1.0 / width) + 1e-06)
        pre_gate = acc_gate[half] * inv_rms
        active[half] = (pre_gate / (1.0 + jnp.exp(-pre_gate)) * (acc_up[half] * inv_rms)).astype(BF16)
        weight[half] = 1.0 / (1.0 + jnp.exp(-acc_logit[half] * inv_rms))
        if (m, half) == (0, 0):
            weight_copies[2].wait()

    def part_copies(m, half, c):
        return [
            remote(
                partial.at[m, half, c, k + 1], partner_part.at[m, half, c, k],
                part_send.at[m, half, c, k], part_recv.at[m, half, c], across_x[k],
            )
            for k in range(3)
        ]

    def step_d(m, half, c):
        part = jnp.dot(active[half], down[:, pl.ds(c * chunk, chunk)], preferred_element_type=F32) * weight[half, :, 0:1]
        partial[m, half, c] = part.astype(BF16).reshape(4, HALF, 2, chunk)
        for copy in part_copies(m, half, c):
            copy.start()

    def step_s(m, half, c):
        landed(partner_part.at[m, half, c], part_recv.at[m, half, c])

        def rows_of(ref):
            return ref[...].reshape(2 * HALF, chunk).astype(F32)

        own = rows_of(partial.at[m, half, c, 0]) + rows_of(partner_part.at[m, half, c, 1])
        other = rows_of(partner_part.at[m, half, c, 0]) + rows_of(partner_part.at[m, half, c, 2])
        back[m, half, c, :, pl.ds(pair, 1)] = own.astype(BF16).reshape(HALF, 1, 2, chunk)
        back[m, half, c, :, pl.ds(1 - pair, 1)] = other.astype(BF16).reshape(HALF, 1, 2, chunk)
        if half == 0:
            pltpu.make_async_copy(back.at[m, 0, c, OWN], home.at[m, c, zy], home_own.at[m, c]).start()
        each_peer(
            half,
            lambda i, there, thence: remote(
                back.at[m, half, c, i], home.at[m, c, zy], home_send.at[m, half, c], home_recv.at[m, half, c], at_x(thence)
            ).start(),
        )

    def pass_on(m, c):
        piece = (m, slice(None), pl.ds(c * chunk, chunk))
        return remote(result.at[piece], hidden.at[piece], pass_sem.at[m], hidden_sem.at[m, c], {"section": 1})

    def out_copy(m, c):
        piece = (m, slice(None), pl.ds(c * chunk, chunk))
        return pltpu.make_async_copy(result.at[piece], out_hbm.at[piece], out_sem.at[m, c])

    def step_c(m, c):
        for half in HALVES:
            half_landed(home.at[m, c], half, home_recv.at[m, half, c], home_own.at[m, c])
        span = pl.ds(c * chunk, chunk)
        spread = jnp.dot(unplace[m], home[m, c].reshape(slots, chunk), preferred_element_type=F32)
        result[m, :, span] = (hidden[m, :, span].astype(F32) + spread).astype(BF16)
        pl.when(section == 0)(lambda: pass_on(m, c).start())
        out_copy(m, c).start()

    steps = dict(N=step_n, M=step_m, X=step_x, G=step_g, A=step_a, D=step_d, S=step_s, C=step_c)

    def run(names):
        for letter, numbers, only in parse(names):
            step = functools.partial(steps[letter], *numbers)
            if only in "ab":
                pl.when(section == "ab".index(only))(step)
            else:
                step()

    begin = ORDER.index("G000")
    run(FIRST)
    pass_shares()
    run(ORDER[:begin])
    collect_shares()
    run(ORDER[begin:])

    landed(shares.at[pl.ds(0, PLANE - 1)], share_send.at[0])
    for copy in share_copies:
        copy.wait_send()
    for m in range(MB):
        pl.when(section == 0)(functools.partial(landed, result.at[m], pass_sem.at[m]))
        for c in ALL:
            landed(outgo.at[m, c, pl.ds(0, PLANE - 1)], out_send.at[m, c])
            for half in HALVES:
                for copy in share_rows(m, half, c) + part_copies(m, half, c):
                    copy.wait_send()
                landed(back.at[m, half, c, pl.ds(0, HALF - 1 + half)], home_send.at[m, half, c])
            out_copy(m, c).wait()


def on_device(tokens_in, route_ids, norm_gain, router, gate_proj, up_proj, down_proj):
    micro_count, tok_rows, width = tokens_in.shape
    units = gate_proj.shape[2]
    chunk = width // CHUNKS
    ids = route_ids.reshape(micro_count, tok_rows)
    any_space = pl.BlockSpec(memory_space=pl.ANY)
    dma = pltpu.SemaphoreType.DMA
    grid = (MB, 2, CHUNKS)
    out = pl.pallas_call(
        kernel,
        name="routed_experts",
        out_shape=jax.ShapeDtypeStruct((micro_count, tok_rows, width), BF16),
        in_specs=[any_space] * 7,
        out_specs=any_space,
        scratch_shapes=[
            pltpu.VMEM((MB, tok_rows), jnp.int32),
            pltpu.VMEM(norm_gain.shape, BF16),
            pltpu.VMEM(router.shape[1:], BF16),
            pltpu.VMEM((PLANE, 2, 2, LANES), BF16),
            pltpu.VMEM((MB, tok_rows, width), BF16),
            pltpu.VMEM((MB, tok_rows, width), BF16),
            pltpu.VMEM((width, units), BF16),
            pltpu.VMEM((width, units), BF16),
            pltpu.VMEM((units, width), BF16),
            pltpu.VMEM((MB, 4 * PLANE, tok_rows), BF16),
            pltpu.VMEM((MB, tok_rows, 4 * PLANE), BF16),
            pltpu.VMEM((PLANE, 2, 2, LANES), BF16),
            pltpu.VMEM((4, PLANE, 2, LANES), BF16),
            pltpu.VMEM((8, width), F32),
            pltpu.VMEM((LANES, width), BF16),
            pltpu.VMEM((MB, CHUNKS, PLANE, 2, 2, chunk), BF16),
            pltpu.VMEM(grid + (HALF, 2, 2, chunk), BF16),
            pltpu.VMEM(grid + (3, HALF, 2, chunk), BF16),
            pltpu.VMEM((2, 8 * HALF, units), F32),
            pltpu.VMEM((2, 8 * HALF, units), F32),
            pltpu.VMEM((2, 8 * HALF, LANES), F32),
            pltpu.VMEM((2, 8 * HALF, LANES), F32),
            pltpu.VMEM((2, 8 * HALF, LANES), F32),
            pltpu.VMEM((2, 8 * HALF, units), BF16),
            pltpu.VMEM(grid + (4, HALF, 2, chunk), BF16),
            pltpu.VMEM(grid + (3, HALF, 2, chunk), BF16),
            pltpu.VMEM(grid + (HALF, 2, 2, chunk), BF16),
            pltpu.VMEM((MB, CHUNKS, PLANE, 2, 2, chunk), BF16),
            dma((3,)), dma((3,)), dma((MB, CHUNKS)), dma((MB, CHUNKS)), dma((MB,)), dma((MB, CHUNKS)), dma((MB, CHUNKS)),
            dma((MB, CHUNKS)), dma(grid), dma(grid + (3,)), dma(grid), dma(grid + (3,)), dma(grid), dma(grid), dma(grid),
            dma((1,)), dma((1,)), dma((3,)), dma((1,)),
        ],
        compiler_params=pltpu.CompilerParams(
            collective_id=0, has_side_effects=True, vmem_limit_bytes=VMEM_BYTES
        ),
    )(ids, norm_gain, router, tokens_in, gate_proj, up_proj, down_proj)
    return out[None]


def solution(mesh):
    return jax.shard_map(
        on_device,
        mesh=mesh,
        in_specs=(
            P(None, "expert", None),
            P("section", None, "expert", None),
            P("section", "expert"),
            P("section", "expert", None),
            P("section", None, "expert"),
            P("section", None, "expert"),
            P("section", "expert", None),
        ),
        out_specs=P("section", None, "expert", None),
        check_vma=False,
    )
```

```python
import functools

import jax
import jax.numpy as jnp
from jax import lax
from jax.experimental import pallas as pl
from jax.experimental.pallas import tpu as pltpu
from jax.sharding import PartitionSpec as P

MESH = pl.DeviceIdType.MESH
HE = 1024
MB = 2
RING_X, RING_Y, RING_Z = 4, 4, 8
PLANE = RING_Y * RING_Z
CHUNKS = 4
VMEM_BYTES = 64 * 1024 * 1024
BF16 = jnp.bfloat16
F32 = jnp.float32
LANES = 128

ALL = tuple(range(CHUNKS))
HALVES = (0, 1)
HALF = PLANE // 2
OWN = HALF - RING_Y
FIRST = (
    "N00a", "N01a", "N02a", "N03a", "M00a", "M01a", "M02a", "M03a",
)
ORDER = (
    "N00b", "N01b", "M00b", "M01b", "N02b", "N03b", "M02b", "M03b", "N10a", "N11a", "N12a", "N13a", "X000", "X001",
    "M10a", "M11a", "X002a", "X003a", "M12a", "M13a", "X010", "X011", "X002b", "X003b", "G000", "G001", "G010b",
    "G011b", "G002", "G003", "A00", "X012", "X013", "D000", "D001", "D002", "D003", "G010a", "G011a", "G012", "G013",
    "A01", "D010", "D011", "D012", "D013", "N10b", "N11b", "M10b", "M11b", "N12b", "N13b", "M12b", "M13b", "X100",
    "X101", "X110b", "X111b", "X102", "X103", "X110a", "X111a", "S000", "S001", "S002", "S003", "X112a", "X113a",
    "S010", "S011", "S012", "S013", "X112b", "X113b", "G100", "G101", "G110b", "G111b", "G102", "G103", "A10", "D100",
    "D101", "D102", "D103", "C00a", "C01a", "C02a", "C03a", "G110a", "G111a", "G112", "G113", "A11", "D110", "D111",
    "D112", "D113", "S100", "S101", "S102", "S103", "S110", "S111", "S112", "S113", "C00b", "C01b", "C02b", "C03b",
    "C10", "C11", "C12", "C13",
)


def parse(names):
    return [(name[0], [int(digit) for digit in name[1:] if digit.isdigit()], name[-1]) for name in names]


def landed(ref, sem):
    pltpu.make_async_copy(ref, ref, sem).wait()


def kernel(
    ids_hbm, gain_hbm, router_hbm, tokens_ref, gate_hbm, up_hbm, down_hbm, out_hbm,
    ids_ref, gain_ref, router_ref, spread_ref, hidden, result, gate, up, down, place, unplace, shares, shares_all, shared, selector,
    outgo, arrive, across, acc_gate, acc_up, acc_logit, acc_square, weight, active, partial, partner_part, back, home,
    small_sem, weight_sem, hidden_sem, out_sem, pass_sem, own_sem, home_own,
    out_send, out_recv, x_send, x_recv, part_send, part_recv, home_send, home_recv,
    share_send, share_recv, share_x_send, share_x_recv,
):
    section = lax.axis_index("section")
    me = lax.axis_index("expert")
    x = lax.rem(me, RING_X)
    zy = me // RING_X
    y = lax.rem(zy, RING_Y)
    z = zy // RING_Y
    pair = x // 2
    partner = x + 1 - 2 * lax.rem(x, 2)
    adjacent = 3 - x
    far = lax.rem(x + 2, RING_X)
    tok_rows, width = hidden.shape[1], hidden.shape[2]
    chunk = width // CHUNKS
    slots = 4 * PLANE
    across_x = [{"expert": zy * RING_X + q} for q in (adjacent, partner, far)]

    def each_peer(half, act):
        def plane(k, dz, first):
            for dy in range(first, RING_Y):
                there = lax.rem(z + dz, RING_Z) * RING_Y + lax.rem(y + dy, RING_Y)
                thence = lax.rem(z + RING_Z - dz, RING_Z) * RING_Y + lax.rem(y + RING_Y - dy, RING_Y)
                act(k * RING_Y + dy, there, thence)

        def body(k, carry):
            far_first = jnp.where(k < 2, 3 + 2 * k, 6 * k - 11) if half else jnp.where(k == 0, 4, 4 * k - 2)
            plane(k, far_first, 0)
            return carry

        lax.fori_loop(0, RING_Z // 2 - 1 + half, body, 0)
        if half == 0:
            plane(RING_Z // 2 - 1, 0, 1)

    def remote(src, dst, send_sem, recv_sem, who):
        return pltpu.make_async_remote_copy(
            src_ref=src, dst_ref=dst, send_sem=send_sem, recv_sem=recv_sem,
            device_id=who, device_id_type=MESH,
        )

    def at_x(there):
        return {"expert": there * RING_X + x}

    def half_landed(dst, half, recv_sem, local_sem):
        landed(dst.at[pl.ds(0, HALF - 1 + half)], recv_sem)
        if half == 0:
            landed(dst.at[0], local_sem)

    weight_copies = [
        pltpu.make_async_copy(gate_hbm.at[0], gate, weight_sem.at[0]),
        pltpu.make_async_copy(up_hbm.at[0], up, weight_sem.at[1]),
        pltpu.make_async_copy(down_hbm.at[0], down, weight_sem.at[2]),
    ]

    ids_copy = pltpu.make_async_copy(ids_hbm, ids_ref, small_sem.at[0])
    gain_copy = pltpu.make_async_copy(gain_hbm, gain_ref, small_sem.at[1])
    router_copy = pltpu.make_async_copy(router_hbm.at[0], router_ref, small_sem.at[2])
    for copy in (ids_copy, gain_copy, router_copy):
        copy.start()

    @pl.when(section == 0)
    def _():
        for m in range(MB):
            for c in ALL:
                piece = (m, slice(None), pl.ds(c * chunk, chunk))
                pltpu.make_async_copy(tokens_ref.at[piece], hidden.at[piece], hidden_sem.at[m, c]).start()

    for copy in weight_copies:
        copy.start()

    barrier = pltpu.get_barrier_semaphore()

    for half in HALVES:
        each_peer(
            half,
            lambda i, there, thence: pl.semaphore_signal(
                barrier, inc=1, device_id=at_x(there), device_id_type=MESH
            ),
        )
    for who in across_x + [{"section": 1 - section}]:
        pl.semaphore_signal(barrier, inc=1, device_id=who, device_id_type=MESH)

    ids_copy.wait()
    row_at = lax.broadcasted_iota(jnp.int32, (tok_rows, tok_rows), 0)
    col_at = lax.broadcasted_iota(jnp.int32, (tok_rows, tok_rows), 1)
    for m in range(MB):
        ids_row = ids_ref[pl.ds(m, 1), :]
        ids_mat = jnp.broadcast_to(ids_row, (tok_rows, tok_rows))
        ids_col = jnp.sum(jnp.where(row_at == col_at, ids_mat, 0), axis=1, keepdims=True)
        same = ids_mat == ids_col
        rank_row = jnp.sum(jnp.where(same & (row_at < col_at), 1, 0), axis=0, keepdims=True)
        rank_col = jnp.sum(jnp.where(same & (col_at < row_at), 1, 0), axis=1, keepdims=True)
        target_row = 2 * ids_row + rank_row
        target_col = 2 * ids_col + rank_col
        slot_at = lax.broadcasted_iota(jnp.int32, (slots, tok_rows), 0)
        place[m] = jnp.where(slot_at == target_row, 1.0, 0.0).astype(BF16)
        slot_at = lax.broadcasted_iota(jnp.int32, (tok_rows, slots), 1)
        unplace[m] = jnp.where(slot_at == target_col, 1.0, 0.0).astype(BF16)

    share_width = width // (RING_X * PLANE)
    column_at = lax.broadcasted_iota(jnp.int32, (1, width), 1)
    column_device = (column_at * ((1 << 18) // share_width + 1)) >> 18
    column_entry = column_at - column_device * share_width
    entry_at = lax.broadcasted_iota(jnp.int32, (LANES, width), 0)
    selector[...] = jnp.where(entry_at == column_entry, 1.0, 0.0).astype(BF16)

    gain_copy.wait()
    router_copy.wait()
    rows, columns = 4 * PLANE, LANES
    widen = jnp.where(
        lax.broadcasted_iota(jnp.int32, (columns, share_width), 0) == lax.broadcasted_iota(jnp.int32, (columns, share_width), 1),
        1.0, 0.0,
    ).astype(BF16)
    router_wide = jnp.dot(widen, router_ref[...], preferred_element_type=F32).astype(BF16)
    gain_rows = jnp.broadcast_to(gain_ref[...], (8, share_width))
    gain_wide = lax.dot_general(gain_rows, widen, (((1,), (1,)), ((), ())), preferred_element_type=F32)
    experts = router_ref.shape[1]
    row_at = lax.broadcasted_iota(jnp.int32, (rows, experts), 0)
    expert_at = lax.broadcasted_iota(jnp.int32, (rows, experts), 1)
    expert_rows = jnp.where(row_at == 2 * expert_at + 1, 1.0, 0.0).astype(BF16)
    router_rows = lax.dot_general(expert_rows, router_wide, (((1,), (1,)), ((), ())), preferred_element_type=F32)
    kind = lax.rem(lax.broadcasted_iota(jnp.int32, (rows, columns), 0), 2)
    spread = jnp.where(kind == 0, gain_wide[0:1, :], router_rows)
    spread_ref[...] = spread.astype(BF16).reshape(PLANE, 2, 2, LANES)
    pl.semaphore_wait(barrier, PLANE + 3)
    shares[pl.ds(zy, 1)] = spread_ref[pl.ds(zy, 1)]
    for half in HALVES:
        each_peer(
            half,
            lambda i, there, thence: remote(
                spread_ref.at[there], shares.at[zy], share_send.at[0], share_recv.at[0], at_x(there)
            ).start(),
        )

    def x_copies(src_of, dst, send_sems, recv_sem):
        return [remote(src_of(k), dst.at[k], send_sems.at[k], recv_sem, across_x[k]) for k in range(3)]

    share_copies = x_copies(
        lambda k: shares.at[:, pair if k == 1 else 1 - pair], shares_all.at[pl.ds(1, 3)], share_x_send, share_x_recv.at[0]
    )

    def pass_shares():
        landed(shares.at[pl.ds(0, PLANE - 1)], share_recv.at[0])
        for copy in share_copies:
            copy.start()
        shares_all[0] = shares[:, pl.ds(pair, 1)].reshape(PLANE, 2, LANES)

    def collect_shares():
        landed(shares_all.at[pl.ds(1, 3)], share_x_recv.at[0])
        blocks = shares_all[...].reshape(8 * PLANE, LANES)
        row = lax.broadcasted_iota(jnp.int32, (8 * PLANE, 1), 0)
        block = row // (2 * PLANE)
        row_x = jnp.where(block == 0, x, jnp.where(block == 1, adjacent, jnp.where(block == 2, partner, far)))
        row_device = lax.rem(row // 2, PLANE) * RING_X + row_x
        kind = lax.rem(lax.broadcasted_iota(jnp.int32, (8, 8 * PLANE), 1), 2)
        kinds = jnp.where(kind == lax.broadcasted_iota(jnp.int32, (8, 8 * PLANE), 0), 1.0, 0.0).astype(BF16)
        for c in ALL:
            span = pl.ds(c * chunk, chunk)
            entries = jnp.dot(blocks, selector[:, span], preferred_element_type=F32)
            device_of = (
                (lax.broadcasted_iota(jnp.int32, (1, chunk), 1) + c * chunk) * ((1 << 18) // share_width + 1)
            ) >> 18
            picked = jnp.where(row_device == device_of, entries, 0.0).astype(BF16)
            shared[:, span] = jnp.dot(kinds, picked, preferred_element_type=F32)

    def step_n(m, c):
        span = pl.ds(c * chunk, chunk)
        landed(hidden.at[m, :, span], hidden_sem.at[m, c])
        rows = jnp.dot(place[m], hidden[m, :, span], preferred_element_type=F32).astype(BF16)
        outgo[m, c] = rows.reshape(PLANE, 2, 2, chunk)
        pltpu.make_async_copy(outgo.at[m, c, zy], arrive.at[m, 0, c, OWN], own_sem.at[m, c]).start()
        send_half(m, 0, c)

    def send_half(m, half, c):
        each_peer(
            half,
            lambda i, there, thence: remote(
                outgo.at[m, c, there], arrive.at[m, half, c, i], out_send.at[m, c], out_recv.at[m, half, c], at_x(there)
            ).start(),
        )

    def step_m(m, c):
        send_half(m, 1, c)

    def share_rows(m, half, c):
        return x_copies(
            lambda k: arrive.at[m, half, c, :, pair if k == 1 else 1 - pair],
            across.at[m, half, c], x_send.at[m, half, c], x_recv.at[m, half, c],
        )

    def step_x(m, half, c):
        half_landed(arrive.at[m, half, c], half, out_recv.at[m, half, c], own_sem.at[m, c])
        for copy in reversed(share_rows(m, half, c)):
            copy.start()

    def step_g(m, half, c):
        if (m, half, c) == (0, 0, 0):
            weight_copies[0].wait()
            weight_copies[1].wait()
        landed(across.at[m, half, c], x_recv.at[m, half, c])
        span = pl.ds(c * chunk, chunk)
        own = arrive[m, half, c, :, pl.ds(pair, 1)].reshape(2 * HALF, chunk)
        rows = jnp.concatenate([own, across[m, half, c].reshape(6 * HALF, chunk)], axis=0)
        square = jnp.zeros((8 * HALF, LANES), F32)
        for lane in range(0, chunk, LANES):
            piece = rows[:, lane:lane + LANES].astype(F32)
            square += piece * piece
        rows = rows * shared[0:1, span].astype(BF16)
        pre_gate = jnp.dot(rows, gate[span, :], preferred_element_type=F32)
        pre_up = jnp.dot(rows, up[span, :], preferred_element_type=F32)
        column = jnp.broadcast_to(shared[1:2, span], (LANES, chunk)).astype(BF16)
        logit = lax.dot_general(rows, column, (((1,), (1,)), ((), ())), preferred_element_type=F32)
        if c == 0:
            acc_gate[half], acc_up[half], acc_logit[half], acc_square[half] = pre_gate, pre_up, logit, square
        else:
            acc_gate[half] += pre_gate
            acc_up[half] += pre_up
            acc_logit[half] += logit
            acc_square[half] += square

    def step_a(m, half):
        inv_rms = lax.rsqrt(jnp.sum(acc_square[half], axis=1, keepdims=True) * (1.0 / width) + 1e-06)
        pre_gate = acc_gate[half] * inv_rms
        active[half] = (pre_gate / (1.0 + jnp.exp(-pre_gate)) * (acc_up[half] * inv_rms)).astype(BF16)
        weight[half] = 1.0 / (1.0 + jnp.exp(-acc_logit[half] * inv_rms))
        if (m, half) == (0, 0):
            weight_copies[2].wait()

    def part_copies(m, half, c):
        return [
            remote(
                partial.at[m, half, c, k + 1], partner_part.at[m, half, c, k],
                part_send.at[m, half, c, k], part_recv.at[m, half, c], across_x[k],
            )
            for k in range(3)
        ]

    def step_d(m, half, c):
        part = jnp.dot(active[half], down[:, pl.ds(c * chunk, chunk)], preferred_element_type=F32) * weight[half, :, 0:1]
        partial[m, half, c] = part.astype(BF16).reshape(4, HALF, 2, chunk)
        for copy in reversed(part_copies(m, half, c)):
            copy.start()

    def step_s(m, half, c):
        landed(partner_part.at[m, half, c], part_recv.at[m, half, c])

        def rows_of(ref):
            return ref[...].reshape(2 * HALF, chunk).astype(F32)

        own = rows_of(partial.at[m, half, c, 0]) + rows_of(partner_part.at[m, half, c, 1])
        other = rows_of(partner_part.at[m, half, c, 0]) + rows_of(partner_part.at[m, half, c, 2])
        back[m, half, c, :, pl.ds(pair, 1)] = own.astype(BF16).reshape(HALF, 1, 2, chunk)
        back[m, half, c, :, pl.ds(1 - pair, 1)] = other.astype(BF16).reshape(HALF, 1, 2, chunk)
        if half == 0:
            pltpu.make_async_copy(back.at[m, 0, c, OWN], home.at[m, c, zy], home_own.at[m, c]).start()
        each_peer(
            half,
            lambda i, there, thence: remote(
                back.at[m, half, c, i], home.at[m, c, zy], home_send.at[m, half, c], home_recv.at[m, half, c], at_x(thence)
            ).start(),
        )

    def pass_on(m, c):
        piece = (m, slice(None), pl.ds(c * chunk, chunk))
        return remote(result.at[piece], hidden.at[piece], pass_sem.at[m], hidden_sem.at[m, c], {"section": 1})

    def out_copy(m, c):
        piece = (m, slice(None), pl.ds(c * chunk, chunk))
        return pltpu.make_async_copy(result.at[piece], out_hbm.at[piece], out_sem.at[m, c])

    def step_c(m, c):
        for half in HALVES:
            half_landed(home.at[m, c], half, home_recv.at[m, half, c], home_own.at[m, c])
        span = pl.ds(c * chunk, chunk)
        spread = jnp.dot(unplace[m], home[m, c].reshape(slots, chunk), preferred_element_type=F32)
        result[m, :, span] = (hidden[m, :, span].astype(F32) + spread).astype(BF16)
        pl.when(section == 0)(lambda: pass_on(m, c).start())
        out_copy(m, c).start()

    steps = dict(N=step_n, M=step_m, X=step_x, G=step_g, A=step_a, D=step_d, S=step_s, C=step_c)

    def run(names):
        for letter, numbers, only in parse(names):
            step = functools.partial(steps[letter], *numbers)
            if only in "ab":
                pl.when(section == "ab".index(only))(step)
            else:
                step()

    begin = ORDER.index("G000")
    run(FIRST)
    pass_shares()
    run(ORDER[:begin])
    collect_shares()
    run(ORDER[begin:])

    landed(shares.at[pl.ds(0, PLANE - 1)], share_send.at[0])
    for copy in share_copies:
        copy.wait_send()
    for m in range(MB):
        pl.when(section == 0)(functools.partial(landed, result.at[m], pass_sem.at[m]))
        for c in ALL:
            landed(outgo.at[m, c, pl.ds(0, PLANE - 1)], out_send.at[m, c])
            for half in HALVES:
                for copy in share_rows(m, half, c) + part_copies(m, half, c):
                    copy.wait_send()
                landed(back.at[m, half, c, pl.ds(0, HALF - 1 + half)], home_send.at[m, half, c])
            out_copy(m, c).wait()


def on_device(tokens_in, route_ids, norm_gain, router, gate_proj, up_proj, down_proj):
    micro_count, tok_rows, width = tokens_in.shape
    units = gate_proj.shape[2]
    chunk = width // CHUNKS
    ids = route_ids.reshape(micro_count, tok_rows)
    any_space = pl.BlockSpec(memory_space=pl.ANY)
    dma = pltpu.SemaphoreType.DMA
    grid = (MB, 2, CHUNKS)
    out = pl.pallas_call(
        kernel,
        name="routed_experts",
        out_shape=jax.ShapeDtypeStruct((micro_count, tok_rows, width), BF16),
        in_specs=[any_space] * 7,
        out_specs=any_space,
        scratch_shapes=[
            pltpu.VMEM((MB, tok_rows), jnp.int32),
            pltpu.VMEM(norm_gain.shape, BF16),
            pltpu.VMEM(router.shape[1:], BF16),
            pltpu.VMEM((PLANE, 2, 2, LANES), BF16),
            pltpu.VMEM((MB, tok_rows, width), BF16),
            pltpu.VMEM((MB, tok_rows, width), BF16),
            pltpu.VMEM((width, units), BF16),
            pltpu.VMEM((width, units), BF16),
            pltpu.VMEM((units, width), BF16),
            pltpu.VMEM((MB, 4 * PLANE, tok_rows), BF16),
            pltpu.VMEM((MB, tok_rows, 4 * PLANE), BF16),
            pltpu.VMEM((PLANE, 2, 2, LANES), BF16),
            pltpu.VMEM((4, PLANE, 2, LANES), BF16),
            pltpu.VMEM((8, width), F32),
            pltpu.VMEM((LANES, width), BF16),
            pltpu.VMEM((MB, CHUNKS, PLANE, 2, 2, chunk), BF16),
            pltpu.VMEM(grid + (HALF, 2, 2, chunk), BF16),
            pltpu.VMEM(grid + (3, HALF, 2, chunk), BF16),
            pltpu.VMEM((2, 8 * HALF, units), F32),
            pltpu.VMEM((2, 8 * HALF, units), F32),
            pltpu.VMEM((2, 8 * HALF, LANES), F32),
            pltpu.VMEM((2, 8 * HALF, LANES), F32),
            pltpu.VMEM((2, 8 * HALF, LANES), F32),
            pltpu.VMEM((2, 8 * HALF, units), BF16),
            pltpu.VMEM(grid + (4, HALF, 2, chunk), BF16),
            pltpu.VMEM(grid + (3, HALF, 2, chunk), BF16),
            pltpu.VMEM(grid + (HALF, 2, 2, chunk), BF16),
            pltpu.VMEM((MB, CHUNKS, PLANE, 2, 2, chunk), BF16),
            dma((3,)), dma((3,)), dma((MB, CHUNKS)), dma((MB, CHUNKS)), dma((MB,)), dma((MB, CHUNKS)), dma((MB, CHUNKS)),
            dma((MB, CHUNKS)), dma(grid), dma(grid + (3,)), dma(grid), dma(grid + (3,)), dma(grid), dma(grid), dma(grid),
            dma((1,)), dma((1,)), dma((3,)), dma((1,)),
        ],
        compiler_params=pltpu.CompilerParams(
            collective_id=0, has_side_effects=True, vmem_limit_bytes=VMEM_BYTES
        ),
    )(ids, norm_gain, router, tokens_in, gate_proj, up_proj, down_proj)
    return out[None]


def solution(mesh):
    return jax.shard_map(
        on_device,
        mesh=mesh,
        in_specs=(
            P(None, "expert", None),
            P("section", None, "expert", None),
            P("section", "expert"),
            P("section", "expert", None),
            P("section", None, "expert"),
            P("section", None, "expert"),
            P("section", "expert", None),
        ),
        out_specs=P("section", None, "expert", None),
        check_vma=False,
    )
```

```python
import functools

import jax
import jax.numpy as jnp
from jax import lax
from jax.experimental import pallas as pl
from jax.experimental.pallas import tpu as pltpu
from jax.sharding import PartitionSpec as P

MESH = pl.DeviceIdType.MESH
HE = 1024
MB = 2
RING_X, RING_Y, RING_Z = 4, 4, 8
FAR_Y = (2, 1, 3, 0)
PLANE = RING_Y * RING_Z
CHUNKS = 4
VMEM_BYTES = 64 * 1024 * 1024
BF16 = jnp.bfloat16
F32 = jnp.float32
LANES = 128

ALL = tuple(range(CHUNKS))
HALVES = (0, 1)
HALF = PLANE // 2
OWN = HALF - RING_Y
FIRST = (
    "N00a", "N01a", "N02a", "N03a", "M00a", "M01a", "M02a", "M03a",
)
ORDER = (
    "N00b", "N01b", "M00b", "M01b", "N02b", "N03b", "M02b", "M03b", "N10a", "N11a", "N12a", "N13a", "X000", "X001",
    "M10a", "M11a", "X002a", "X003a", "M12a", "M13a", "X010", "X011", "X002b", "X003b", "G000", "G001", "G010b",
    "G011b", "G002", "G003", "A00", "X012", "X013", "D000", "D001", "D002", "D003", "G010a", "G011a", "G012", "G013",
    "A01", "D010", "D011", "D012", "D013", "N10b", "N11b", "M10b", "M11b", "N12b", "N13b", "M12b", "M13b", "X100",
    "X101", "X110b", "X111b", "X102", "X103", "X110a", "X111a", "S000", "S001", "S002", "S003", "X112a", "X113a",
    "S010", "S011", "S012", "S013", "X112b", "X113b", "G100", "G101", "G110b", "G111b", "G102", "G103", "A10", "D100",
    "D101", "D102", "D103", "C00a", "C01a", "C02a", "C03a", "G110a", "G111a", "G112", "G113", "A11", "D110", "D111",
    "D112", "D113", "S100", "S101", "S102", "S103", "S110", "S111", "S112", "S113", "C00b", "C01b", "C02b", "C03b",
    "C10", "C11", "C12", "C13",
)


def parse(names):
    return [(name[0], [int(digit) for digit in name[1:] if digit.isdigit()], name[-1]) for name in names]


def landed(ref, sem):
    pltpu.make_async_copy(ref, ref, sem).wait()


def kernel(
    ids_hbm, gain_hbm, router_hbm, tokens_ref, gate_hbm, up_hbm, down_hbm, out_hbm,
    ids_ref, gain_ref, router_ref, spread_ref, hidden, result, gate, up, down, place, unplace, shares, shares_all, shared, selector,
    outgo, arrive, across, acc_gate, acc_up, acc_logit, acc_square, weight, active, partial, partner_part, back, home,
    small_sem, weight_sem, hidden_sem, out_sem, pass_sem, own_sem, home_own,
    out_send, out_recv, x_send, x_recv, part_send, part_recv, home_send, home_recv,
    share_send, share_recv, share_x_send, share_x_recv,
):
    section = lax.axis_index("section")
    me = lax.axis_index("expert")
    x = lax.rem(me, RING_X)
    zy = me // RING_X
    y = lax.rem(zy, RING_Y)
    z = zy // RING_Y
    pair = x // 2
    partner = x + 1 - 2 * lax.rem(x, 2)
    adjacent = 3 - x
    far = lax.rem(x + 2, RING_X)
    tok_rows, width = hidden.shape[1], hidden.shape[2]
    chunk = width // CHUNKS
    slots = 4 * PLANE
    across_x = [{"expert": zy * RING_X + q} for q in (adjacent, partner, far)]

    def each_peer(half, act):
        def plane(k, dz, first):
            for dy in [d for d in FAR_Y if d >= first]:
                there = lax.rem(z + dz, RING_Z) * RING_Y + lax.rem(y + dy, RING_Y)
                thence = lax.rem(z + RING_Z - dz, RING_Z) * RING_Y + lax.rem(y + RING_Y - dy, RING_Y)
                act(k * RING_Y + dy, there, thence)

        def body(k, carry):
            far_first = jnp.where(k < 2, 3 + 2 * k, 6 * k - 11) if half else jnp.where(k == 0, 4, 4 * k - 2)
            plane(k, far_first, 0)
            return carry

        lax.fori_loop(0, RING_Z // 2 - 1 + half, body, 0)
        if half == 0:
            plane(RING_Z // 2 - 1, 0, 1)

    def remote(src, dst, send_sem, recv_sem, who):
        return pltpu.make_async_remote_copy(
            src_ref=src, dst_ref=dst, send_sem=send_sem, recv_sem=recv_sem,
            device_id=who, device_id_type=MESH,
        )

    def at_x(there):
        return {"expert": there * RING_X + x}

    def half_landed(dst, half, recv_sem, local_sem):
        landed(dst.at[pl.ds(0, HALF - 1 + half)], recv_sem)
        if half == 0:
            landed(dst.at[0], local_sem)

    weight_copies = [
        pltpu.make_async_copy(gate_hbm.at[0], gate, weight_sem.at[0]),
        pltpu.make_async_copy(up_hbm.at[0], up, weight_sem.at[1]),
        pltpu.make_async_copy(down_hbm.at[0], down, weight_sem.at[2]),
    ]

    ids_copy = pltpu.make_async_copy(ids_hbm, ids_ref, small_sem.at[0])
    gain_copy = pltpu.make_async_copy(gain_hbm, gain_ref, small_sem.at[1])
    router_copy = pltpu.make_async_copy(router_hbm.at[0], router_ref, small_sem.at[2])
    for copy in (ids_copy, gain_copy, router_copy):
        copy.start()

    @pl.when(section == 0)
    def _():
        for m in range(MB):
            for c in ALL:
                piece = (m, slice(None), pl.ds(c * chunk, chunk))
                pltpu.make_async_copy(tokens_ref.at[piece], hidden.at[piece], hidden_sem.at[m, c]).start()

    for copy in weight_copies:
        copy.start()

    barrier = pltpu.get_barrier_semaphore()

    for half in HALVES:
        each_peer(
            half,
            lambda i, there, thence: pl.semaphore_signal(
                barrier, inc=1, device_id=at_x(there), device_id_type=MESH
            ),
        )
    for who in across_x + [{"section": 1 - section}]:
        pl.semaphore_signal(barrier, inc=1, device_id=who, device_id_type=MESH)

    ids_copy.wait()
    row_at = lax.broadcasted_iota(jnp.int32, (tok_rows, tok_rows), 0)
    col_at = lax.broadcasted_iota(jnp.int32, (tok_rows, tok_rows), 1)
    for m in range(MB):
        ids_row = ids_ref[pl.ds(m, 1), :]
        ids_mat = jnp.broadcast_to(ids_row, (tok_rows, tok_rows))
        ids_col = jnp.sum(jnp.where(row_at == col_at, ids_mat, 0), axis=1, keepdims=True)
        same = ids_mat == ids_col
        rank_row = jnp.sum(jnp.where(same & (row_at < col_at), 1, 0), axis=0, keepdims=True)
        rank_col = jnp.sum(jnp.where(same & (col_at < row_at), 1, 0), axis=1, keepdims=True)
        target_row = 2 * ids_row + rank_row
        target_col = 2 * ids_col + rank_col
        slot_at = lax.broadcasted_iota(jnp.int32, (slots, tok_rows), 0)
        place[m] = jnp.where(slot_at == target_row, 1.0, 0.0).astype(BF16)
        slot_at = lax.broadcasted_iota(jnp.int32, (tok_rows, slots), 1)
        unplace[m] = jnp.where(slot_at == target_col, 1.0, 0.0).astype(BF16)

    share_width = width // (RING_X * PLANE)
    column_at = lax.broadcasted_iota(jnp.int32, (1, width), 1)
    column_device = (column_at * ((1 << 18) // share_width + 1)) >> 18
    column_entry = column_at - column_device * share_width
    entry_at = lax.broadcasted_iota(jnp.int32, (LANES, width), 0)
    selector[...] = jnp.where(entry_at == column_entry, 1.0, 0.0).astype(BF16)

    gain_copy.wait()
    router_copy.wait()
    rows, columns = 4 * PLANE, LANES
    widen = jnp.where(
        lax.broadcasted_iota(jnp.int32, (columns, share_width), 0) == lax.broadcasted_iota(jnp.int32, (columns, share_width), 1),
        1.0, 0.0,
    ).astype(BF16)
    router_wide = jnp.dot(widen, router_ref[...], preferred_element_type=F32).astype(BF16)
    gain_rows = jnp.broadcast_to(gain_ref[...], (8, share_width))
    gain_wide = lax.dot_general(gain_rows, widen, (((1,), (1,)), ((), ())), preferred_element_type=F32)
    experts = router_ref.shape[1]
    row_at = lax.broadcasted_iota(jnp.int32, (rows, experts), 0)
    expert_at = lax.broadcasted_iota(jnp.int32, (rows, experts), 1)
    expert_rows = jnp.where(row_at == 2 * expert_at + 1, 1.0, 0.0).astype(BF16)
    router_rows = lax.dot_general(expert_rows, router_wide, (((1,), (1,)), ((), ())), preferred_element_type=F32)
    kind = lax.rem(lax.broadcasted_iota(jnp.int32, (rows, columns), 0), 2)
    spread = jnp.where(kind == 0, gain_wide[0:1, :], router_rows)
    spread_ref[...] = spread.astype(BF16).reshape(PLANE, 2, 2, LANES)
    pl.semaphore_wait(barrier, PLANE + 3)
    shares[pl.ds(zy, 1)] = spread_ref[pl.ds(zy, 1)]
    for half in HALVES:
        each_peer(
            half,
            lambda i, there, thence: remote(
                spread_ref.at[there], shares.at[zy], share_send.at[0], share_recv.at[0], at_x(there)
            ).start(),
        )

    def x_copies(src_of, dst, send_sems, recv_sem):
        return [remote(src_of(k), dst.at[k], send_sems.at[k], recv_sem, across_x[k]) for k in range(3)]

    share_copies = x_copies(
        lambda k: shares.at[:, pair if k == 1 else 1 - pair], shares_all.at[pl.ds(1, 3)], share_x_send, share_x_recv.at[0]
    )

    def pass_shares():
        landed(shares.at[pl.ds(0, PLANE - 1)], share_recv.at[0])
        for copy in share_copies:
            copy.start()
        shares_all[0] = shares[:, pl.ds(pair, 1)].reshape(PLANE, 2, LANES)

    def collect_shares():
        landed(shares_all.at[pl.ds(1, 3)], share_x_recv.at[0])
        blocks = shares_all[...].reshape(8 * PLANE, LANES)
        row = lax.broadcasted_iota(jnp.int32, (8 * PLANE, 1), 0)
        block = row // (2 * PLANE)
        row_x = jnp.where(block == 0, x, jnp.where(block == 1, adjacent, jnp.where(block == 2, partner, far)))
        row_device = lax.rem(row // 2, PLANE) * RING_X + row_x
        kind = lax.rem(lax.broadcasted_iota(jnp.int32, (8, 8 * PLANE), 1), 2)
        kinds = jnp.where(kind == lax.broadcasted_iota(jnp.int32, (8, 8 * PLANE), 0), 1.0, 0.0).astype(BF16)
        for c in ALL:
            span = pl.ds(c * chunk, chunk)
            entries = jnp.dot(blocks, selector[:, span], preferred_element_type=F32)
            device_of = (
                (lax.broadcasted_iota(jnp.int32, (1, chunk), 1) + c * chunk) * ((1 << 18) // share_width + 1)
            ) >> 18
            picked = jnp.where(row_device == device_of, entries, 0.0).astype(BF16)
            shared[:, span] = jnp.dot(kinds, picked, preferred_element_type=F32)

    def step_n(m, c):
        span = pl.ds(c * chunk, chunk)
        landed(hidden.at[m, :, span], hidden_sem.at[m, c])
        rows = jnp.dot(place[m], hidden[m, :, span], preferred_element_type=F32).astype(BF16)
        outgo[m, c] = rows.reshape(PLANE, 2, 2, chunk)
        pltpu.make_async_copy(outgo.at[m, c, zy], arrive.at[m, 0, c, OWN], own_sem.at[m, c]).start()
        send_half(m, 0, c)

    def send_half(m, half, c):
        each_peer(
            half,
            lambda i, there, thence: remote(
                outgo.at[m, c, there], arrive.at[m, half, c, i], out_send.at[m, c], out_recv.at[m, half, c], at_x(there)
            ).start(),
        )

    def step_m(m, c):
        send_half(m, 1, c)

    def share_rows(m, half, c):
        return x_copies(
            lambda k: arrive.at[m, half, c, :, pair if k == 1 else 1 - pair],
            across.at[m, half, c], x_send.at[m, half, c], x_recv.at[m, half, c],
        )

    def step_x(m, half, c):
        half_landed(arrive.at[m, half, c], half, out_recv.at[m, half, c], own_sem.at[m, c])
        for copy in reversed(share_rows(m, half, c)):
            copy.start()

    def step_g(m, half, c):
        if (m, half, c) == (0, 0, 0):
            weight_copies[0].wait()
            weight_copies[1].wait()
        landed(across.at[m, half, c], x_recv.at[m, half, c])
        span = pl.ds(c * chunk, chunk)
        own = arrive[m, half, c, :, pl.ds(pair, 1)].reshape(2 * HALF, chunk)
        rows = jnp.concatenate([own, across[m, half, c].reshape(6 * HALF, chunk)], axis=0)
        square = jnp.zeros((8 * HALF, LANES), F32)
        for lane in range(0, chunk, LANES):
            piece = rows[:, lane:lane + LANES].astype(F32)
            square += piece * piece
        rows = rows * shared[0:1, span].astype(BF16)
        pre_gate = jnp.dot(rows, gate[span, :], preferred_element_type=F32)
        pre_up = jnp.dot(rows, up[span, :], preferred_element_type=F32)
        column = jnp.broadcast_to(shared[1:2, span], (LANES, chunk)).astype(BF16)
        logit = lax.dot_general(rows, column, (((1,), (1,)), ((), ())), preferred_element_type=F32)
        if c == 0:
            acc_gate[half], acc_up[half], acc_logit[half], acc_square[half] = pre_gate, pre_up, logit, square
        else:
            acc_gate[half] += pre_gate
            acc_up[half] += pre_up
            acc_logit[half] += logit
            acc_square[half] += square

    def step_a(m, half):
        inv_rms = lax.rsqrt(jnp.sum(acc_square[half], axis=1, keepdims=True) * (1.0 / width) + 1e-06)
        pre_gate = acc_gate[half] * inv_rms
        active[half] = (pre_gate / (1.0 + jnp.exp(-pre_gate)) * (acc_up[half] * inv_rms)).astype(BF16)
        weight[half] = 1.0 / (1.0 + jnp.exp(-acc_logit[half] * inv_rms))
        if (m, half) == (0, 0):
            weight_copies[2].wait()

    def part_copies(m, half, c):
        return [
            remote(
                partial.at[m, half, c, k + 1], partner_part.at[m, half, c, k],
                part_send.at[m, half, c, k], part_recv.at[m, half, c], across_x[k],
            )
            for k in range(3)
        ]

    def step_d(m, half, c):
        part = jnp.dot(active[half], down[:, pl.ds(c * chunk, chunk)], preferred_element_type=F32) * weight[half, :, 0:1]
        partial[m, half, c] = part.astype(BF16).reshape(4, HALF, 2, chunk)
        for copy in reversed(part_copies(m, half, c)):
            copy.start()

    def step_s(m, half, c):
        landed(partner_part.at[m, half, c], part_recv.at[m, half, c])

        def rows_of(ref):
            return ref[...].reshape(2 * HALF, chunk).astype(F32)

        own = rows_of(partial.at[m, half, c, 0]) + rows_of(partner_part.at[m, half, c, 1])
        other = rows_of(partner_part.at[m, half, c, 0]) + rows_of(partner_part.at[m, half, c, 2])
        back[m, half, c, :, pl.ds(pair, 1)] = own.astype(BF16).reshape(HALF, 1, 2, chunk)
        back[m, half, c, :, pl.ds(1 - pair, 1)] = other.astype(BF16).reshape(HALF, 1, 2, chunk)
        if half == 0:
            pltpu.make_async_copy(back.at[m, 0, c, OWN], home.at[m, c, zy], home_own.at[m, c]).start()
        each_peer(
            half,
            lambda i, there, thence: remote(
                back.at[m, half, c, i], home.at[m, c, zy], home_send.at[m, half, c], home_recv.at[m, half, c], at_x(thence)
            ).start(),
        )

    def pass_on(m, c):
        piece = (m, slice(None), pl.ds(c * chunk, chunk))
        return remote(result.at[piece], hidden.at[piece], pass_sem.at[m], hidden_sem.at[m, c], {"section": 1})

    def out_copy(m, c):
        piece = (m, slice(None), pl.ds(c * chunk, chunk))
        return pltpu.make_async_copy(result.at[piece], out_hbm.at[piece], out_sem.at[m, c])

    def step_c(m, c):
        for half in HALVES:
            half_landed(home.at[m, c], half, home_recv.at[m, half, c], home_own.at[m, c])
        span = pl.ds(c * chunk, chunk)
        spread = jnp.dot(unplace[m], home[m, c].reshape(slots, chunk), preferred_element_type=F32)
        result[m, :, span] = (hidden[m, :, span].astype(F32) + spread).astype(BF16)
        pl.when(section == 0)(lambda: pass_on(m, c).start())
        out_copy(m, c).start()

    steps = dict(N=step_n, M=step_m, X=step_x, G=step_g, A=step_a, D=step_d, S=step_s, C=step_c)

    def run(names):
        for letter, numbers, only in parse(names):
            step = functools.partial(steps[letter], *numbers)
            if only in "ab":
                pl.when(section == "ab".index(only))(step)
            else:
                step()

    begin = ORDER.index("G000")
    run(FIRST)
    pass_shares()
    run(ORDER[:begin])
    collect_shares()
    run(ORDER[begin:])

    landed(shares.at[pl.ds(0, PLANE - 1)], share_send.at[0])
    for copy in share_copies:
        copy.wait_send()
    for m in range(MB):
        pl.when(section == 0)(functools.partial(landed, result.at[m], pass_sem.at[m]))
        for c in ALL:
            landed(outgo.at[m, c, pl.ds(0, PLANE - 1)], out_send.at[m, c])
            for half in HALVES:
                for copy in share_rows(m, half, c) + part_copies(m, half, c):
                    copy.wait_send()
                landed(back.at[m, half, c, pl.ds(0, HALF - 1 + half)], home_send.at[m, half, c])
            out_copy(m, c).wait()


def on_device(tokens_in, route_ids, norm_gain, router, gate_proj, up_proj, down_proj):
    micro_count, tok_rows, width = tokens_in.shape
    units = gate_proj.shape[2]
    chunk = width // CHUNKS
    ids = route_ids.reshape(micro_count, tok_rows)
    any_space = pl.BlockSpec(memory_space=pl.ANY)
    dma = pltpu.SemaphoreType.DMA
    grid = (MB, 2, CHUNKS)
    out = pl.pallas_call(
        kernel,
        name="routed_experts",
        out_shape=jax.ShapeDtypeStruct((micro_count, tok_rows, width), BF16),
        in_specs=[any_space] * 7,
        out_specs=any_space,
        scratch_shapes=[
            pltpu.VMEM((MB, tok_rows), jnp.int32),
            pltpu.VMEM(norm_gain.shape, BF16),
            pltpu.VMEM(router.shape[1:], BF16),
            pltpu.VMEM((PLANE, 2, 2, LANES), BF16),
            pltpu.VMEM((MB, tok_rows, width), BF16),
            pltpu.VMEM((MB, tok_rows, width), BF16),
            pltpu.VMEM((width, units), BF16),
            pltpu.VMEM((width, units), BF16),
            pltpu.VMEM((units, width), BF16),
            pltpu.VMEM((MB, 4 * PLANE, tok_rows), BF16),
            pltpu.VMEM((MB, tok_rows, 4 * PLANE), BF16),
            pltpu.VMEM((PLANE, 2, 2, LANES), BF16),
            pltpu.VMEM((4, PLANE, 2, LANES), BF16),
            pltpu.VMEM((8, width), F32),
            pltpu.VMEM((LANES, width), BF16),
            pltpu.VMEM((MB, CHUNKS, PLANE, 2, 2, chunk), BF16),
            pltpu.VMEM(grid + (HALF, 2, 2, chunk), BF16),
            pltpu.VMEM(grid + (3, HALF, 2, chunk), BF16),
            pltpu.VMEM((2, 8 * HALF, units), F32),
            pltpu.VMEM((2, 8 * HALF, units), F32),
            pltpu.VMEM((2, 8 * HALF, LANES), F32),
            pltpu.VMEM((2, 8 * HALF, LANES), F32),
            pltpu.VMEM((2, 8 * HALF, LANES), F32),
            pltpu.VMEM((2, 8 * HALF, units), BF16),
            pltpu.VMEM(grid + (4, HALF, 2, chunk), BF16),
            pltpu.VMEM(grid + (3, HALF, 2, chunk), BF16),
            pltpu.VMEM(grid + (HALF, 2, 2, chunk), BF16),
            pltpu.VMEM((MB, CHUNKS, PLANE, 2, 2, chunk), BF16),
            dma((3,)), dma((3,)), dma((MB, CHUNKS)), dma((MB, CHUNKS)), dma((MB,)), dma((MB, CHUNKS)), dma((MB, CHUNKS)),
            dma((MB, CHUNKS)), dma(grid), dma(grid + (3,)), dma(grid), dma(grid + (3,)), dma(grid), dma(grid), dma(grid),
            dma((1,)), dma((1,)), dma((3,)), dma((1,)),
        ],
        compiler_params=pltpu.CompilerParams(
            collective_id=0, has_side_effects=True, vmem_limit_bytes=VMEM_BYTES
        ),
    )(ids, norm_gain, router, tokens_in, gate_proj, up_proj, down_proj)
    return out[None]


def solution(mesh):
    return jax.shard_map(
        on_device,
        mesh=mesh,
        in_specs=(
            P(None, "expert", None),
            P("section", None, "expert", None),
            P("section", "expert"),
            P("section", "expert", None),
            P("section", None, "expert"),
            P("section", None, "expert"),
            P("section", "expert", None),
        ),
        out_specs=P("section", None, "expert", None),
        check_vma=False,
    )
```
